256 devices in a mesh: tm: 8 (over z), seq: 32 (over x, y, core).
Axes of the slice: x: 4, y: 4, z: 8, core: 2. Of those that a mesh axis runs over, the one named last changes fastest.
Arguments:
- query_in: bfloat16 [32768, 512], P(('tm', 'seq')), may hold values from -30 to 30
- key_in: bfloat16 [32768, 128], P(('tm', 'seq')), may hold values from -6 to 6
- value_in: bfloat16 [32768, 128], P(('tm', 'seq')), may hold values from -6 to 6
- clean_keys: bfloat16 [32768, 128], P(('tm', 'seq')), may hold values from -6 to 6
- clean_values: bfloat16 [32768, 128], P(('tm', 'seq')), may hold values from -6 to 6
- timestep: int32 [8], P('tm'), may hold values from 0 to 999
- mod_table: float32 [1000, 512], replicated, may hold values from 0.5 to 3
- out_grad: bfloat16 [32768, 512], P(('tm', 'seq')), may hold values from -6 to 6
Outputs:
- gated_out: float32 [32768, 512], P(('tm', 'seq'))
- query_grad: float32 [32768, 512], P(('tm', 'seq'))
- key_grad: float32 [32768, 128], P(('tm', 'seq'))
- value_grad: float32 [32768, 128], P(('tm', 'seq'))
The draws below stay inside these ranges and needn't reach their ends.
All inputs are finite; a program needn't handle non-finite values.
Results may differ from the reference program's by a relative error of at most 0.04.
Values may be sent and summed in bfloat16 or wider, within the bound.
A program may use at most 128 MiB of HBM per device.

```python
import math
import jax
import jax.numpy as jnp
from jax import lax

QH = 4
HD = 128
NSTEPS = 1000
GROUP_TOK = 4096
GROUPS = 8
TOKENS = 32768


def shared_rows(key):
    base_keys = jnp.clip(jax.random.normal(key, (TOKENS, HD), jnp.float32), -6.0, 6.0)
    return base_keys


def draw_key_in(key, part):
    base_keys = shared_rows(key)
    keys_out = base_keys
    return keys_out.astype(jnp.bfloat16)


def draw_query_in(key, part):
    key = jax.random.fold_in(key, 5)
    queries = jnp.clip(2.5 * jax.random.normal(key, (TOKENS, QH * HD), jnp.float32), -12.0, 12.0)
    return queries.astype(jnp.bfloat16)


def set_ends(array, key, least, largest):
    extent = array.shape
    index_at = [jax.random.randint(jax.random.fold_in(key, axis), (), 0, extent[axis]) for axis in range(len(extent))]
    array = array.at[tuple(index_at)].set(least)
    longest = extent.index(max(extent))
    index_at[longest] = (index_at[longest] + 1) % extent[longest]
    return array.at[tuple(index_at)].set(largest)


def block_scale(stream_key, dims, split, least, high):
    def one(axis_at, blocks):
        draws = jax.random.uniform(jax.random.fold_in(jax.random.fold_in(stream_key, 6), axis_at), (blocks,), jnp.float32, least / len(split), high / len(split))
        return jnp.repeat(jnp.exp(draws), dims[axis_at] // blocks).reshape((-1,) + (1,) * (len(dims) - axis_at - 1))

    loudness = one(*split[0])
    for cut in split[1:]:
        loudness = loudness * one(*cut)
    return loudness


def bell_draw(key, extent, deviation, bound, cuts=(), dtype=jnp.bfloat16):
    array = deviation * jax.random.normal(key, extent, jnp.float32)
    if cuts:
        array = array * block_scale(key, extent, cuts, -0.22, 0.18)
    return jnp.clip(array, -bound, bound).astype(dtype)


def setup_inputs(seed: int = 0) -> dict:
    keys = jax.random.split(jax.random.key(seed), 9)
    query_in = draw_query_in(jax.random.fold_in(keys[8], 71), 0)
    key_in = draw_key_in(jax.random.fold_in(keys[8], 71), 0)
    value_in = bell_draw(keys[2], (TOKENS, HD), 1.0, 6.0, ((0, 256),))
    clean_keys = bell_draw(keys[3], (TOKENS, HD), 1.0, 6.0, ((0, 256),))
    clean_values = bell_draw(keys[4], (TOKENS, HD), 1.0, 6.0, ((0, 256),))
    timestep = set_ends(jax.random.randint(keys[5], (GROUPS,), 0, NSTEPS), jax.random.fold_in(keys[5], 1), 0, NSTEPS - 1).astype(jnp.int32)
    mod_table = jnp.clip(jax.random.uniform(keys[6], (NSTEPS, QH * HD), jnp.float32, 0.5, 3.0), 0.5, 3.0)
    out_grad = bell_draw(keys[7], (TOKENS, QH * HD), 1.0, 6.0, ((0, 256),))
    return {"query_in": query_in, "key_in": key_in, "value_in": value_in, "clean_keys": clean_keys, "clean_values": clean_values, "timestep": timestep, "mod_table": mod_table, "out_grad": out_grad}


def reference(query_in, key_in, value_in, clean_keys, clean_values, timestep, mod_table, out_grad):
    group_span = GROUP_TOK
    width = QH * HD
    score_scale = 1.0 / math.sqrt(HD)
    row_block = math.gcd(group_span * QH, 1024)
    block_count = group_span * QH // row_block
    outs_list, qgrad_list, kgrad_list, vgrad_list = ([], [], [], [])
    for group_index in range(GROUPS):
        lower = group_index * group_span
        upper = lower + group_span
        keys_all = jnp.concatenate([clean_keys[:lower], key_in[lower:upper]], 0)
        values_all = jnp.concatenate([clean_values[:lower], value_in[lower:upper]], 0)
        gain = mod_table[timestep[group_index]][None, :].astype(jnp.float32)
        query_rows = query_in[lower:upper].reshape(group_span * QH, HD)
        grads = (gain * out_grad[lower:upper].astype(jnp.float32)).astype(jnp.bfloat16)
        grad_rows = grads.reshape(group_span * QH, HD)

        def one_block(carried, pair):
            key_acc, value_acc = carried
            query_blk, grad_blk = pair
            scores = jnp.dot(query_blk, keys_all.T, preferred_element_type=jnp.float32) * score_scale
            peak = lax.optimization_barrier(jnp.max(scores, axis=1))
            expo = jnp.exp(scores - peak[:, None])
            total = lax.optimization_barrier(jnp.sum(expo, axis=1))
            attended = (jnp.dot(expo.astype(jnp.bfloat16), values_all, preferred_element_type=jnp.float32) / total[:, None]).astype(jnp.bfloat16)
            lse = peak + jnp.log(total)
            delta = lax.optimization_barrier(jnp.sum(grad_blk.astype(jnp.float32) * attended.astype(jnp.float32), axis=1))
            probs = jnp.exp(scores - lse[:, None])
            prob_half = probs.astype(jnp.bfloat16)
            dprob = jnp.dot(grad_blk, values_all.T, preferred_element_type=jnp.float32)
            dscore = (probs * (dprob - delta[:, None]) * score_scale).astype(jnp.bfloat16)
            qgrad = jnp.dot(dscore, keys_all, preferred_element_type=jnp.float32)
            key_acc = key_acc + jnp.dot(dscore[:, -group_span:].T, query_blk, preferred_element_type=jnp.float32)
            value_acc = value_acc + jnp.dot(prob_half[:, -group_span:].T, grad_blk, preferred_element_type=jnp.float32)
            return ((key_acc, value_acc), (attended, qgrad))
        start_acc = (jnp.zeros((group_span, HD), jnp.float32), jnp.zeros((group_span, HD), jnp.float32))
        (key_acc, value_acc), (attended, qgrad) = lax.scan(one_block, start_acc, (query_rows.reshape(block_count, row_block, HD), grad_rows.reshape(block_count, row_block, HD)))
        attended = attended.reshape(group_span, width)
        outs_list.append(gain * attended.astype(jnp.float32))
        qgrad_list.append(qgrad.reshape(group_span, width))
        kgrad_list.append(key_acc)
        vgrad_list.append(value_acc)
    return (jnp.concatenate(outs_list, 0), jnp.concatenate(qgrad_list, 0), jnp.concatenate(kgrad_list, 0), jnp.concatenate(vgrad_list, 0))
```

```python
import math

import jax
import jax.numpy as jnp
from jax import lax
from jax.experimental import pallas as pl
from jax.experimental.pallas import tpu as pltpu
from jax.sharding import PartitionSpec as P

MESH = pl.DeviceIdType.MESH
HALF = jnp.bfloat16
FULL = jnp.float32
SIDE = 4
PLANES = 8
TOK = 128
HD = 128
HEADS = 4
ROWS = HEADS * TOK
BOTH = 2 * ROWS
CUT = TOK // 2
REGION = SIDE * SIDE * CUT
LINE = SIDE * CUT
BK = REGION // 2
LEAD1 = 6
LEAD2 = 4


def dot(a, b):
    return lax.dot_general(a, b, (((1,), (0,)), ((), ())), preferred_element_type=FULL)


def dot_tn(a, b):
    return lax.dot_general(a, b, (((0,), (0,)), ((), ())), preferred_element_type=FULL)


def fold(a, op):
    return op(a.reshape(a.shape[0] // 8, 8, a.shape[1]), axis=0)


def kernel(
    timestep, query, key_in, value_in, clean_keys, clean_values, mod_table, out_grad,
    gated, query_grad, key_grad, value_grad,
    kv, clean, table, qg, qg_sib, qt, gt, q_rows, g_rows,
    s_buf, e_buf, x_buf, m_buf, al_buf, l_buf, o1, o2,
    ml, ml_sib, o1_sib, o2_sib, stats, stats_sib,
    part, own_part, rs1, rs2_out, rs2,
    table_sem, core_send, core_recv, z_send, z_recv, s1_send, s1_recv, s2_send, s2_recv,
    rs1_send, rs1_recv, rs2_send, rs2_recv,
):
    scale = 1.0 / math.sqrt(HD)
    to_log2 = scale * math.log2(math.e)
    z = lax.axis_index("tm")
    seq = lax.axis_index("seq")
    core = lax.rem(seq, 2)
    y = lax.rem(seq // 2, SIDE)
    x = seq // (2 * SIDE)
    regions = 2 * (z + 1)

    def chip(dx, dy):
        px = lax.rem(x + dx, SIDE)
        py = lax.rem(y + dy, SIDE)
        return (z, (px * SIDE + py) * 2 + core)

    sibling = (z, (x * SIDE + y) * 2 + 1 - core)

    def plane(pz):
        return (pz, seq)

    def remote(src, dst, send, recv, device):
        return pltpu.make_async_remote_copy(
            src_ref=src, dst_ref=dst, send_sem=send, recv_sem=recv,
            device_id=device, device_id_type=MESH,
        )

    def along_line(r, d):
        p = lax.rem(r, 2)
        return chip((1 - p) * d, p * d)

    def across_lines(r, d):
        p = lax.rem(r, 2)
        return chip(p * d, (1 - p) * d)

    def place(r):
        p = lax.rem(r, 2)
        return p * x + (1 - p) * y, p * y + (1 - p) * x

    table_copy = pltpu.make_async_copy(mod_table, table, table_sem)
    table_copy.start()

    barrier = pltpu.get_barrier_semaphore()
    for d in range(1, SIDE):
        pl.semaphore_signal(barrier, inc=1, device_id=chip(d, 0), device_id_type=MESH)
        pl.semaphore_signal(barrier, inc=1, device_id=chip(0, d), device_id_type=MESH)
    for d in range(1, PLANES):
        pl.semaphore_signal(
            barrier, inc=1, device_id=plane(lax.rem(z + d, PLANES)), device_id_type=MESH
        )
    pl.semaphore_signal(barrier, inc=1, device_id=sibling, device_id_type=MESH)

    for p in range(2):
        u, v = place(p)
        start = pl.multiple_of(u * LINE + v * CUT, CUT)
        rows = pl.ds(p * CUT, CUT)
        kv[p, pl.ds(start, CUT), :HD] = value_in[rows, :]
        kv[p, pl.ds(start, CUT), HD:] = key_in[rows, :]
    clean[:, :HD] = clean_values[...]
    clean[:, HD:] = clean_keys[...]

    pl.semaphore_wait(barrier, 2 * (SIDE - 1) + PLANES)

    def stage1(r):
        u, v = place(r)
        piece = kv.at[r, pl.ds(pl.multiple_of(u * LINE + v * CUT, CUT), CUT)]
        for d in range(1, SIDE):
            remote(piece, piece, s1_send.at[r], s1_recv.at[r], along_line(r, d)).start()

    def wait_part(r, sem, keys, sending):
        block = kv.at[r, pl.ds(0, keys)]
        pltpu.make_async_copy(block, block, sem.at[r]).wait()

    def stage2(r):
        wait_part(r, s1_recv, (SIDE - 1) * CUT, False)
        u, _ = place(r)
        line = kv.at[r, pl.ds(pl.multiple_of(u * LINE, LINE), LINE)]
        for d in range(1, SIDE):
            remote(line, line, s2_send.at[r], s2_recv.at[r], across_lines(r, d)).start()

    def clean_copy(r, device):
        p = lax.rem(r, 2)
        u, v = place(r)
        return remote(
            clean.at[pl.ds(pl.multiple_of(p * CUT, CUT), CUT)],
            kv.at[r, pl.ds(pl.multiple_of(u * LINE + v * CUT, CUT), CUT)],
            z_send.at[r], z_recv.at[r], device,
        )

    def clean_stage1(r):
        clean_copy(r, plane(z)).wait_recv()
        stage1(r)

    def wait_region(r):
        wait_part(r, s2_recv, (SIDE - 1) * LINE, False)

    stage1(0)
    stage1(1)

    table_copy.wait()
    gain = table[pl.ds(timestep[0], 1), :]
    qg[0] = query[...]
    qg[1] = (gain * out_grad[...].astype(FULL)).astype(HALF)
    share_rows = remote(qg, qg_sib, core_send.at[0], core_recv.at[0], sibling)
    share_rows.start()

    def send_clean(d, carry):
        @pl.when(z + d < PLANES)
        def _():
            for p in range(2):
                clean_copy(2 * d + p, plane(lax.rem(z + d, PLANES))).start()
        return carry

    lax.fori_loop(1, PLANES, send_clean, 0)

    def lay_rows(source, at):
        for h in range(HEADS):
            cols = pl.ds(h * HD, HD)
            rows = pl.ds(at + h * TOK, TOK)
            q_head = source[0, :, cols]
            g_head = source[1, :, cols]
            q_rows[rows, :] = q_head
            g_rows[rows, :] = g_head
            qt[:, rows] = q_head.T
            gt[:, rows] = g_head.T

    lay_rows(qg, 0)
    stage2(0)
    stage2(1)
    share_rows.wait_recv()
    lay_rows(qg_sib, ROWS)

    def lead_stage1(r, carry):
        @pl.when(r < regions)
        def _():
            clean_stage1(r)
        return carry

    def lead_stage2(r, carry):
        @pl.when(r < regions)
        def _():
            stage2(r)
        return carry

    lax.fori_loop(2, LEAD1, lead_stage1, 0)

    l_buf[...] = jnp.zeros_like(l_buf)
    o1[...] = jnp.zeros_like(o1)
    o2[...] = jnp.zeros_like(o2)
    e_buf[1] = jnp.zeros_like(e_buf[1])
    x_buf[1] = jnp.zeros_like(x_buf[1])
    al_buf[...] = jnp.ones_like(al_buf)
    m_buf[...] = jnp.full_like(m_buf, -1e30)

    lax.fori_loop(2, LEAD2, lead_stage2, 0)

    def scores(r, at, parity, j):
        cols = pl.ds(j * ROWS, ROWS)
        s = dot(kv[r, pl.ds(at, BK), HD:], qt[:, cols])
        s_buf[1 - parity, :, cols] = s
        before = m_buf[parity, :, cols]
        top = jnp.max(fold(s, jnp.max), axis=0, keepdims=True) * to_log2
        after = jnp.maximum(before, top)
        m_buf[1 - parity, :, cols] = after
        al_buf[1 - parity, :, cols] = jnp.exp2(before - after)

    def weigh(r, at, parity, j):
        cols = pl.ds(j * ROWS, ROWS)
        e = jnp.exp2(s_buf[parity, :, cols] * to_log2 - m_buf[parity, :1, cols])
        dprob = dot(kv[r, pl.ds(at, BK), :HD], gt[:, cols])
        e_buf[parity, :, cols] = e.astype(HALF)
        x_buf[parity, :, cols] = (e * dprob).astype(HALF)
        l_buf[:, cols] = l_buf[:, cols] * al_buf[parity, :, cols] + fold(e, jnp.sum)

    def gather_sums(r, at, parity, j):
        cols = pl.ds(j * ROWS, ROWS)
        al = al_buf[parity, :1, cols]
        o1[j] = o1[j] * al + dot_tn(kv[r, pl.ds(at, BK), :], e_buf[parity, :, cols])
        o2[j] = o2[j] * al + dot_tn(kv[r, pl.ds(at, BK), HD:], x_buf[parity, :, cols])

    wait_region(0)
    for j in range(2):
        scores(0, 0, 1, j)

    def step(i, carry):
        @pl.when(i + LEAD1 < regions)
        def _():
            clean_stage1(i + LEAD1)

        @pl.when(i + LEAD2 < regions)
        def _():
            stage2(i + LEAD2)

        @pl.when(i + 1 < regions)
        def _():
            wait_region(i + 1)

        last = jnp.maximum(i - 1, 0)
        following = jnp.minimum(i + 1, regions - 1)
        for j in range(2):
            weigh(i, 0, 0, j)
            gather_sums(last, BK, 1, j)
            scores(i, BK, 0, j)
        for j in range(2):
            weigh(i, BK, 1, j)
            gather_sums(i, 0, 0, j)
            scores(following, 0, 1, j)
        return carry

    lax.fori_loop(0, regions, step, 0)
    for j in (1, 0):
        gather_sums(regions - 1, BK, 1, j)
        if j == 1:
            ml[0] = m_buf[1, :, ROWS:]
            ml[1] = l_buf[:, ROWS:]
            shares = [
                remote(ml, ml_sib, core_send.at[1], core_recv.at[1], sibling),
                remote(o1.at[1], o1_sib, core_send.at[2], core_recv.at[2], sibling),
                remote(o2.at[1], o2_sib, core_send.at[3], core_recv.at[3], sibling),
            ]
            for share in shares:
                share.start()

    for share in shares:
        share.wait_recv()
    peak_a = m_buf[1, :1, :ROWS]
    peak_b = ml_sib[0, :1, :]
    peak = jnp.maximum(peak_a, peak_b)
    part_a = jnp.exp2(peak_a - peak)
    part_b = jnp.exp2(peak_b - peak)
    total = part_a * jnp.sum(l_buf[:, :ROWS], axis=0, keepdims=True) + part_b * jnp.sum(
        ml_sib[1], axis=0, keepdims=True
    )
    part_a = part_a / total
    part_b = part_b / total
    attended = (o1[0, :HD, :] * part_a + o1_sib[:HD, :] * part_b).astype(HALF)
    delta = jnp.sum(gt[:, :ROWS].astype(FULL) * attended.astype(FULL), axis=0, keepdims=True)
    stats[0] = jnp.broadcast_to(peak + jnp.log2(total), (8, ROWS))
    stats[1] = jnp.broadcast_to(delta, (8, ROWS))
    share_stats = remote(stats, stats_sib, core_send.at[4], core_recv.at[4], sibling)
    share_stats.start()

    mean_key = o1[0, HD:, :] * part_a + o1_sib[HD:, :] * part_b
    qgrad = (o2[0] * part_a + o2_sib[...] * part_b - delta * mean_key) * scale
    attended = attended.astype(FULL)
    for h in range(HEADS):
        cols = slice(h * HD, (h + 1) * HD)
        gated[:, cols] = gain[:, cols] * attended[:, h * TOK : (h + 1) * TOK].T
        query_grad[:, cols] = qgrad[:, h * TOK : (h + 1) * TOK].T
    share_stats.wait_recv()

    def backward(p, line):
        block = kv[p, pl.ds(pl.multiple_of(line * LINE, LINE), LINE), :]
        lse = jnp.concatenate([stats[0, :1, :], stats_sib[0, :1, :]], axis=1)
        drop = jnp.concatenate([stats[1, :1, :], stats_sib[1, :1, :]], axis=1)
        prob = jnp.exp2(dot(block[:, HD:], qt[...]) * to_log2 - lse)
        dprob = dot(block[:, :HD], gt[...])
        dscore = (prob * (dprob - drop) * scale).astype(HALF)
        vgrad = dot(prob.astype(HALF), g_rows[...])
        kgrad = dot(dscore, q_rows[...])
        return vgrad, kgrad

    def part_copy(p, d):
        return remote(
            part.at[p, d - 1], rs1.at[p, d - 1],
            rs1_send.at[p, d - 1], rs1_recv.at[p, d - 1], across_lines(p, d),
        )

    for d in (2, 1, 3):
        for p in range(2):
            u, _ = place(p)
            vgrad, kgrad = backward(p, lax.rem(u + d, SIDE))
            part[p, d - 1, :, :HD] = vgrad.astype(HALF)
            part[p, d - 1, :, HD:] = kgrad.astype(HALF)
            part_copy(p, d).start()
    for p in range(2):
        u, _ = place(p)
        vgrad, kgrad = backward(p, u)
        own_part[p, :, :HD] = vgrad
        own_part[p, :, HD:] = kgrad

    def piece_copy(p, d):
        _, v = place(p)
        at = pl.multiple_of(lax.rem(v + d, SIDE) * CUT, CUT)
        return remote(
            rs2_out.at[p, pl.ds(at, CUT)], rs2.at[p, d - 1],
            rs2_send.at[p, d - 1], rs2_recv.at[p, d - 1], along_line(p, d),
        )

    for p in range(2):
        for d in range(1, SIDE):
            part_copy(p, d).wait_recv()
        own_part[p] = (
            own_part[p] + rs1[p, 0].astype(FULL) + rs1[p, 1].astype(FULL) + rs1[p, 2].astype(FULL)
        )
        rs2_out[p] = own_part[p].astype(HALF)
        for d in range(1, SIDE):
            piece_copy(p, d).start()
    for p in range(2):
        _, v = place(p)
        for d in range(1, SIDE):
            piece_copy(p, d).wait_recv()
        mine = own_part[p, pl.ds(pl.multiple_of(v * CUT, CUT), CUT), :]
        mine = mine + rs2[p, 0].astype(FULL) + rs2[p, 1].astype(FULL) + rs2[p, 2].astype(FULL)
        value_grad[pl.ds(p * CUT, CUT), :] = mine[:, :HD]
        key_grad[pl.ds(p * CUT, CUT), :] = mine[:, HD:]

    for copy in [share_rows, share_stats] + shares:
        copy.wait_send()
    for p in range(2):
        for d in range(1, SIDE):
            part_copy(p, d).wait_send()
            piece_copy(p, d).wait_send()

    def drain(r, carry):
        wait_part(r, s1_send, (SIDE - 1) * CUT, True)
        wait_part(r, s2_send, (SIDE - 1) * LINE, True)
        return carry

    lax.fori_loop(0, regions, drain, 0)

    def drain_clean(d, carry):
        @pl.when(z + d < PLANES)
        def _():
            for p in range(2):
                clean_copy(2 * d + p, plane(lax.rem(z + d, PLANES))).wait_send()
        return carry

    lax.fori_loop(1, PLANES, drain_clean, 0)


def body(query_in, key_in, value_in, clean_keys, clean_values, timestep, mod_table, out_grad):
    vmem = pl.BlockSpec(memory_space=pltpu.VMEM)
    dma = pltpu.SemaphoreType.DMA
    slots = 2 * PLANES
    return pl.pallas_call(
        kernel,
        name="attend",
        out_shape=[
            jax.ShapeDtypeStruct((TOK, HEADS * HD), FULL),
            jax.ShapeDtypeStruct((TOK, HEADS * HD), FULL),
            jax.ShapeDtypeStruct((TOK, HD), FULL),
            jax.ShapeDtypeStruct((TOK, HD), FULL),
        ],
        in_specs=[pl.BlockSpec(memory_space=pltpu.SMEM)]
        + [vmem] * 5
        + [pl.BlockSpec(memory_space=pl.ANY), vmem],
        out_specs=[vmem] * 4,
        scratch_shapes=[
            pltpu.VMEM((slots, REGION, 2 * HD), HALF),
            pltpu.VMEM((TOK, 2 * HD), HALF),
            pltpu.VMEM(mod_table.shape, FULL),
            pltpu.VMEM((2, TOK, HEADS * HD), HALF),
            pltpu.VMEM((2, TOK, HEADS * HD), HALF),
            pltpu.VMEM((HD, BOTH), HALF),
            pltpu.VMEM((HD, BOTH), HALF),
            pltpu.VMEM((BOTH, HD), HALF),
            pltpu.VMEM((BOTH, HD), HALF),
            pltpu.VMEM((2, BK, BOTH), FULL),
            pltpu.VMEM((2, BK, BOTH), HALF),
            pltpu.VMEM((2, BK, BOTH), HALF),
            pltpu.VMEM((2, 8, BOTH), FULL),
            pltpu.VMEM((2, 8, BOTH), FULL),
            pltpu.VMEM((8, BOTH), FULL),
            pltpu.VMEM((2, 2 * HD, ROWS), FULL),
            pltpu.VMEM((2, HD, ROWS), FULL),
            pltpu.VMEM((2, 8, ROWS), FULL),
            pltpu.VMEM((2, 8, ROWS), FULL),
            pltpu.VMEM((2 * HD, ROWS), FULL),
            pltpu.VMEM((HD, ROWS), FULL),
            pltpu.VMEM((2, 8, ROWS), FULL),
            pltpu.VMEM((2, 8, ROWS), FULL),
            pltpu.VMEM((2, SIDE - 1, LINE, 2 * HD), HALF),
            pltpu.VMEM((2, LINE, 2 * HD), FULL),
            pltpu.VMEM((2, SIDE - 1, LINE, 2 * HD), HALF),
            pltpu.VMEM((2, LINE, 2 * HD), HALF),
            pltpu.VMEM((2, SIDE - 1, CUT, 2 * HD), HALF),
            dma,
            dma((5,)), dma((5,)),
            dma((slots,)), dma((slots,)),
            dma((slots,)), dma((slots,)),
            dma((slots,)), dma((slots,)),
            dma((2, SIDE - 1)), dma((2, SIDE - 1)),
            dma((2, SIDE - 1)), dma((2, SIDE - 1)),
        ],
        compiler_params=pltpu.CompilerParams(
            collective_id=0, has_side_effects=True, vmem_limit_bytes=50 * 2**20
        ),
    )(timestep, query_in, key_in, value_in, clean_keys, clean_values, mod_table, out_grad)


def solution(mesh):
    assert mesh.shape["tm"] == PLANES and mesh.shape["seq"] == 2 * SIDE * SIDE
    split = P(("tm", "seq"), None)
    return jax.shard_map(
        body,
        mesh=mesh,
        in_specs=(split, split, split, split, split, P("tm"), P(), split),
        out_specs=(split, split, split, split),
        check_vma=False,
    )
```

```python
import math

import jax
import jax.numpy as jnp
from jax import lax
from jax.experimental import pallas as pl
from jax.experimental.pallas import tpu as pltpu
from jax.sharding import PartitionSpec as P

MESH = pl.DeviceIdType.MESH
HALF = jnp.bfloat16
FULL = jnp.float32
SIDE = 4
PLANES = 8
TOK = 128
HD = 128
HEADS = 4
ROWS = HEADS * TOK
BOTH = 2 * ROWS
CUT = TOK // 2
REGION = SIDE * SIDE * CUT
LINE = SIDE * CUT
BK = REGION // 2


def dot(a, b):
    return lax.dot_general(a, b, (((1,), (0,)), ((), ())), preferred_element_type=FULL)


def dot_tn(a, b):
    return lax.dot_general(a, b, (((0,), (0,)), ((), ())), preferred_element_type=FULL)


def fold(a, op):
    return op(a.reshape(a.shape[0] // 8, 8, a.shape[1]), axis=0)


def kernel(
    timestep, query, key_in, value_in, clean_keys, clean_values, mod_table, out_grad,
    gated, query_grad, key_grad, value_grad,
    kv, clean, table, grad_in, qg, qg_sib, qt, gt, q_rows, g_rows,
    s_buf, e_buf, x_buf, m_buf, al_buf, l_buf, o1, o2,
    ml, ml_sib, o1_sib, o2_sib, stats, stats_sib,
    part, own_part, rs1, rs2_out, rs2,
    in_sem, core_send, core_recv, z_send, z_recv,
    s1_send, s1_recv, up_send, up_recv, down_send, down_recv, s3_send, s3_recv,
    rs1_send, rs1_recv, rs2_send, rs2_recv,
):
    scale = 1.0 / math.sqrt(HD)
    to_log2 = scale * math.log2(math.e)
    z = lax.axis_index("tm")
    seq = lax.axis_index("seq")
    core = lax.rem(seq, 2)
    y = lax.rem(seq // 2, SIDE)
    x = seq // (2 * SIDE)
    regions = 2 * (z + 1)

    def chip(dx, dy):
        px = lax.rem(x + dx, SIDE)
        py = lax.rem(y + dy, SIDE)
        return (z, (px * SIDE + py) * 2 + core)

    sibling = (z, (x * SIDE + y) * 2 + 1 - core)

    def plane(pz):
        return (pz, seq)

    def remote(src, dst, send, recv, device):
        return pltpu.make_async_remote_copy(
            src_ref=src, dst_ref=dst, send_sem=send, recv_sem=recv,
            device_id=device, device_id_type=MESH,
        )

    def along_line(p, d):
        return chip((1 - p) * d, p * d)

    def across_lines(p, d):
        return chip(p * d, (1 - p) * d)

    def place(p):
        return p * x + (1 - p) * y, p * y + (1 - p) * x

    loads = [
        pltpu.make_async_copy(query, qg.at[0], in_sem.at[0]),
        pltpu.make_async_copy(out_grad, grad_in, in_sem.at[1]),
        pltpu.make_async_copy(mod_table, table, in_sem.at[2]),
    ]
    shards = []
    for p in range(2):
        u, v = place(p)
        rows = pl.ds(p * CUT, CUT)
        noisy_at = pl.ds(pl.multiple_of(u * LINE + v * CUT, CUT), CUT)
        for at, (noisy_in, clean_in) in enumerate(
            ((value_in, clean_values), (key_in, clean_keys))
        ):
            cols = pl.ds(at * HD, HD)
            sem = 3 + 4 * p + 2 * at
            shards.append(
                pltpu.make_async_copy(
                    noisy_in.at[rows, :], kv.at[p, noisy_at, cols], in_sem.at[sem]
                )
            )
            shards.append(
                pltpu.make_async_copy(
                    clean_in.at[rows, :], clean.at[p, :, cols], in_sem.at[sem + 1]
                )
            )
    for load in shards + loads:
        load.start()

    barrier = pltpu.get_barrier_semaphore()
    for d in range(1, SIDE):
        pl.semaphore_signal(barrier, inc=1, device_id=chip(d, 0), device_id_type=MESH)
        pl.semaphore_signal(barrier, inc=1, device_id=chip(0, d), device_id_type=MESH)
    for d in range(1, PLANES):
        pl.semaphore_signal(
            barrier, inc=1, device_id=plane(lax.rem(z + d, PLANES)), device_id_type=MESH
        )
    pl.semaphore_signal(barrier, inc=1, device_id=sibling, device_id_type=MESH)
    for load in shards:
        load.wait()
    pl.semaphore_wait(barrier, 2 * (SIDE - 1) + PLANES)

    def arrived(block, sem):
        pltpu.make_async_copy(block, block, sem).wait()

    def piece_at(r):
        u, v = place(lax.rem(r, 2))
        return kv.at[r, pl.ds(pl.multiple_of(u * LINE + v * CUT, CUT), CUT)]

    def gather_line(r):
        piece = piece_at(r)
        for d in range(1, SIDE):
            remote(
                piece, piece, s1_send.at[r], s1_recv.at[r], along_line(lax.rem(r, 2), d)
            ).start()

    for p in range(2):
        gather_line(p)

    def line_at(r, shift):
        u, _ = place(lax.rem(r, 2))
        line = lax.rem(u + shift, SIDE)
        return kv.at[r, pl.ds(pl.multiple_of(line * LINE, LINE), LINE)]

    def half_line_at(r, shift, second):
        u, _ = place(lax.rem(r, 2))
        line = lax.rem(u + shift, SIDE)
        return kv.at[r, pl.ds(pl.multiple_of(line * LINE + second * (LINE // 2), LINE // 2), LINE // 2)]

    def spread(r):
        p = lax.rem(r, 2)
        line = line_at(r, 0)
        remote(line, line, up_send.at[r], up_recv.at[r], across_lines(p, 1)).start()
        remote(line, line, down_send.at[r], down_recv.at[r], across_lines(p, SIDE - 1)).start()

    def pass_on(r):
        p = lax.rem(r, 2)
        arrived(line_at(r, SIDE - 1), up_recv.at[r])
        first = half_line_at(r, SIDE - 1, 0)
        remote(first, first, s3_send.at[r], s3_recv.at[r], across_lines(p, 1)).start()
        arrived(line_at(r, 1), down_recv.at[r])
        second = half_line_at(r, 1, 1)
        remote(second, second, s3_send.at[r], s3_recv.at[r], across_lines(p, SIDE - 1)).start()

    def complete(r):
        arrived(line_at(r, 2), s3_recv.at[r])

    def shard_copy(r):
        return remote(
            clean.at[lax.rem(r, 2)], piece_at(r), z_send.at[r], z_recv.at[r],
            plane(lax.rem(z + r // 2, PLANES)),
        )

    def send_shards(d, carry):
        @pl.when(z + d < PLANES)
        def _():
            for p in range(2):
                shard_copy(2 * d + p).start()
        return carry

    def take_shard(r):
        arrived(piece_at(r), z_recv.at[r])
        gather_line(r)

    def take_line(r):
        arrived(kv.at[r, pl.ds(0, (SIDE - 1) * CUT)], s1_recv.at[r])
        spread(r)

    lax.fori_loop(1, PLANES, send_shards, 0)
    for load in loads:
        load.wait()
    gain = table[pl.ds(timestep[0], 1), :]
    qg[1] = (gain * grad_in[...].astype(FULL)).astype(HALF)
    share_rows = remote(qg, qg_sib, core_send.at[0], core_recv.at[0], sibling)
    share_rows.start()

    def lay_rows(source, at):
        for h in range(HEADS):
            cols = pl.ds(h * HD, HD)
            rows = pl.ds(at + h * TOK, TOK)
            q_head = source[0, :, cols]
            g_head = source[1, :, cols]
            q_rows[rows, :] = q_head
            g_rows[rows, :] = g_head
            qt[:, rows] = q_head.T
            gt[:, rows] = g_head.T

    lay_rows(qg, 0)
    for p in range(2):
        take_line(p)
    share_rows.wait_recv()
    lay_rows(qg_sib, ROWS)

    def lead(low, high, work):
        def one(r, carry):
            @pl.when(r < regions)
            def _():
                work(r)
            return carry

        lax.fori_loop(low, high, one, 0)

    l_buf[...] = jnp.zeros_like(l_buf)
    o1[...] = jnp.zeros_like(o1)
    o2[...] = jnp.zeros_like(o2)
    e_buf[1] = jnp.zeros_like(e_buf[1])
    x_buf[1] = jnp.zeros_like(x_buf[1])
    al_buf[...] = jnp.ones_like(al_buf)
    m_buf[...] = jnp.full_like(m_buf, -1e30)

    def first_block(t):
        i, h = t // 2, lax.rem(t, 2)
        return (2 * i + h, h), (2 * i + 1, 3 * h)

    def second_block(t):
        i, h = t // 2, lax.rem(t, 2)
        return (2 * i, 1 + h), (2 * i + h, 3 - h)

    def rows_of(block, cols):
        return jnp.concatenate([line_at(r, shift)[:, cols] for r, shift in block], axis=0)

    values, keys, all_cols = slice(0, HD), slice(HD, 2 * HD), slice(0, 2 * HD)

    def scores(block, parity, j):
        cols = pl.ds(j * ROWS, ROWS)
        s = dot(rows_of(block, keys), qt[:, cols])
        s_buf[1 - parity, :, cols] = s
        before = m_buf[parity, :, cols]
        top = jnp.max(fold(s, jnp.max), axis=0, keepdims=True) * to_log2
        after = jnp.maximum(before, top)
        m_buf[1 - parity, :, cols] = after
        al_buf[1 - parity, :, cols] = jnp.exp2(before - after)

    def weigh(block, parity, j):
        cols = pl.ds(j * ROWS, ROWS)
        e = jnp.exp2(s_buf[parity, :, cols] * to_log2 - m_buf[parity, :1, cols])
        dprob = dot(rows_of(block, values), gt[:, cols])
        e_buf[parity, :, cols] = e.astype(HALF)
        x_buf[parity, :, cols] = (e * dprob).astype(HALF)
        l_buf[:, cols] = l_buf[:, cols] * al_buf[parity, :, cols] + fold(e, jnp.sum)

    def gather_sums(block, parity, j):
        cols = pl.ds(j * ROWS, ROWS)
        al = al_buf[parity, :1, cols]
        o1[j] = o1[j] * al + dot_tn(rows_of(block, all_cols), e_buf[parity, :, cols])
        o2[j] = o2[j] * al + dot_tn(rows_of(block, keys), x_buf[parity, :, cols])

    def half_step(t, h, j):
        if h == 0:
            weigh(first_block(t), 0, j)
            gather_sums(second_block(jnp.maximum(t - 1, 0)), 1, j)
            scores(second_block(t), 0, j)
        else:
            weigh(second_block(t), 1, j)
            gather_sums(first_block(t), 0, j)
            scores(first_block(jnp.minimum(t + 1, regions - 1)), 1, j)

    def finish_unit(t):
        @pl.when(lax.rem(t, 2) == 1)
        def _():
            complete(t - 1)
            complete(t)

    lead(2, 6, take_shard)
    for j in range(2):
        scores(first_block(0), 1, j)
    for p in range(2):
        pass_on(p)
    lead(2, 4, take_line)

    def step(t, carry):
        finish_unit(t)
        for j in range(2):
            half_step(t, 0, j)
        lead(t + 8 - 2 * jnp.maximum(1 - t, 0), t + 9, take_shard)
        lead(jnp.minimum(2 * t + 4, t + 6), jnp.minimum(2 * t + 6, t + 7), take_line)
        lead(jnp.maximum(jnp.minimum(2 * t, t + 3), 2), jnp.minimum(2 * t + 2, t + 4), pass_on)
        for j in range(2):
            half_step(t, 1, j)
        return carry

    lax.fori_loop(0, regions - 2, step, 0)

    for j in (1, 0):

        def last_step(t, carry):
            if j == 1:
                finish_unit(t)
            half_step(t, 0, j)
            half_step(t, 1, j)
            return carry

        lax.fori_loop(regions - 2, regions, last_step, 0)
        gather_sums(second_block(regions - 1), 1, j)
        if j == 1:
            ml[0] = m_buf[1, :, ROWS:]
            ml[1] = l_buf[:, ROWS:]
            shares = [
                remote(ml, ml_sib, core_send.at[1], core_recv.at[1], sibling),
                remote(o1.at[1], o1_sib, core_send.at[2], core_recv.at[2], sibling),
                remote(o2.at[1], o2_sib, core_send.at[3], core_recv.at[3], sibling),
            ]
            for share in shares:
                share.start()

    for share in shares:
        share.wait_recv()
    peak_a = m_buf[1, :1, :ROWS]
    peak_b = ml_sib[0, :1, :]
    peak = jnp.maximum(peak_a, peak_b)
    part_a = jnp.exp2(peak_a - peak)
    part_b = jnp.exp2(peak_b - peak)
    total = part_a * jnp.sum(l_buf[:, :ROWS], axis=0, keepdims=True) + part_b * jnp.sum(
        ml_sib[1], axis=0, keepdims=True
    )
    part_a = part_a / total
    part_b = part_b / total
    attended = (o1[0, :HD, :] * part_a + o1_sib[:HD, :] * part_b).astype(HALF)
    delta = jnp.sum(gt[:, :ROWS].astype(FULL) * attended.astype(FULL), axis=0, keepdims=True)
    stats[0] = jnp.broadcast_to(peak + jnp.log2(total), (8, ROWS))
    stats[1] = jnp.broadcast_to(delta, (8, ROWS))
    share_stats = remote(stats, stats_sib, core_send.at[4], core_recv.at[4], sibling)
    share_stats.start()

    mean_key = o1[0, HD:, :] * part_a + o1_sib[HD:, :] * part_b
    qgrad = (o2[0] * part_a + o2_sib[...] * part_b - delta * mean_key) * scale
    attended = attended.astype(FULL)
    for h in range(HEADS):
        cols = slice(h * HD, (h + 1) * HD)
        gated[:, cols] = gain[:, cols] * attended[:, h * TOK : (h + 1) * TOK].T
        query_grad[:, cols] = qgrad[:, h * TOK : (h + 1) * TOK].T
    def backward(p, line, cols, lse, drop):
        block = kv[p, pl.ds(pl.multiple_of(line * LINE, LINE), LINE), :]
        prob = jnp.exp2(dot(block[:, HD:], qt[:, cols]) * to_log2 - lse)
        dprob = dot(block[:, :HD], gt[:, cols])
        dscore = (prob * (dprob - drop) * scale).astype(HALF)
        vgrad = dot(prob.astype(HALF), g_rows[cols, :])
        kgrad = dot(dscore, q_rows[cols, :])
        return vgrad, kgrad

    def backward_mine(p, line):
        return backward(p, line, pl.ds(0, ROWS), stats[0, :1, :], stats[1, :1, :])

    def backward_theirs(p, line):
        return backward(p, line, pl.ds(ROWS, ROWS), stats_sib[0, :1, :], stats_sib[1, :1, :])

    def backward_all(p, line):
        lse = jnp.concatenate([stats[0, :1, :], stats_sib[0, :1, :]], axis=1)
        drop = jnp.concatenate([stats[1, :1, :], stats_sib[1, :1, :]], axis=1)
        return backward(p, line, pl.ds(0, BOTH), lse, drop)

    def part_copy(p, d):
        return remote(
            part.at[p, d - 1], rs1.at[p, d - 1],
            rs1_send.at[p, d - 1], rs1_recv.at[p, d - 1], across_lines(p, d),
        )

    early = [backward_mine(p, lax.rem(place(p)[0] + 2, SIDE)) for p in range(2)]
    share_stats.wait_recv()
    for d in (2, 1, 3):
        for p in range(2):
            line = lax.rem(place(p)[0] + d, SIDE)
            if d == 2:
                late = backward_theirs(p, line)
                vgrad, kgrad = early[p][0] + late[0], early[p][1] + late[1]
            else:
                vgrad, kgrad = backward_all(p, line)
            part[p, d - 1, :, :HD] = vgrad.astype(HALF)
            part[p, d - 1, :, HD:] = kgrad.astype(HALF)
            part_copy(p, d).start()
    for p in range(2):
        u, _ = place(p)
        vgrad, kgrad = backward_all(p, u)
        own_part[p, :, :HD] = vgrad
        own_part[p, :, HD:] = kgrad

    def piece_copy(p, d):
        _, v = place(p)
        at = pl.multiple_of(lax.rem(v + d, SIDE) * CUT, CUT)
        return remote(
            rs2_out.at[p, pl.ds(at, CUT)], rs2.at[p, d - 1],
            rs2_send.at[p, d - 1], rs2_recv.at[p, d - 1], along_line(p, d),
        )

    for p in range(2):
        for d in range(1, SIDE):
            part_copy(p, d).wait_recv()
        own_part[p] = (
            own_part[p] + rs1[p, 0].astype(FULL) + rs1[p, 1].astype(FULL) + rs1[p, 2].astype(FULL)
        )
        rs2_out[p] = own_part[p].astype(HALF)
        for d in range(1, SIDE):
            piece_copy(p, d).start()
    for p in range(2):
        _, v = place(p)
        for d in range(1, SIDE):
            piece_copy(p, d).wait_recv()
        mine = own_part[p, pl.ds(pl.multiple_of(v * CUT, CUT), CUT), :]
        mine = mine + rs2[p, 0].astype(FULL) + rs2[p, 1].astype(FULL) + rs2[p, 2].astype(FULL)
        value_grad[pl.ds(p * CUT, CUT), :] = mine[:, :HD]
        key_grad[pl.ds(p * CUT, CUT), :] = mine[:, HD:]

    for copy in [share_rows, share_stats] + shares:
        copy.wait_send()
    for p in range(2):
        for d in range(1, SIDE):
            part_copy(p, d).wait_send()
            piece_copy(p, d).wait_send()

    def drain(r, carry):
        line = line_at(r, 0)
        for sem in (up_send, down_send, s3_send):
            arrived(line, sem.at[r])
        arrived(kv.at[r, pl.ds(0, (SIDE - 1) * CUT)], s1_send.at[r])
        return carry

    lax.fori_loop(0, regions, drain, 0)

    def drain_shards(d, carry):
        @pl.when(z + d < PLANES)
        def _():
            for p in range(2):
                shard_copy(2 * d + p).wait_send()
        return carry

    lax.fori_loop(1, PLANES, drain_shards, 0)


def body(query_in, key_in, value_in, clean_keys, clean_values, timestep, mod_table, out_grad):
    vmem = pl.BlockSpec(memory_space=pltpu.VMEM)
    dma = pltpu.SemaphoreType.DMA
    slots = 2 * PLANES
    return pl.pallas_call(
        kernel,
        name="attend",
        out_shape=[
            jax.ShapeDtypeStruct((TOK, HEADS * HD), FULL),
            jax.ShapeDtypeStruct((TOK, HEADS * HD), FULL),
            jax.ShapeDtypeStruct((TOK, HD), FULL),
            jax.ShapeDtypeStruct((TOK, HD), FULL),
        ],
        in_specs=[pl.BlockSpec(memory_space=pltpu.SMEM)]
        + [pl.BlockSpec(memory_space=pl.ANY)] * 7,
        out_specs=[vmem] * 4,
        scratch_shapes=[
            pltpu.VMEM((slots, REGION, 2 * HD), HALF),
            pltpu.VMEM((2, CUT, 2 * HD), HALF),
            pltpu.VMEM(mod_table.shape, FULL),
            pltpu.VMEM((TOK, HEADS * HD), HALF),
            pltpu.VMEM((2, TOK, HEADS * HD), HALF),
            pltpu.VMEM((2, TOK, HEADS * HD), HALF),
            pltpu.VMEM((HD, BOTH), HALF),
            pltpu.VMEM((HD, BOTH), HALF),
            pltpu.VMEM((BOTH, HD), HALF),
            pltpu.VMEM((BOTH, HD), HALF),
            pltpu.VMEM((2, BK, BOTH), FULL),
            pltpu.VMEM((2, BK, BOTH), HALF),
            pltpu.VMEM((2, BK, BOTH), HALF),
            pltpu.VMEM((2, 8, BOTH), FULL),
            pltpu.VMEM((2, 8, BOTH), FULL),
            pltpu.VMEM((8, BOTH), FULL),
            pltpu.VMEM((2, 2 * HD, ROWS), FULL),
            pltpu.VMEM((2, HD, ROWS), FULL),
            pltpu.VMEM((2, 8, ROWS), FULL),
            pltpu.VMEM((2, 8, ROWS), FULL),
            pltpu.VMEM((2 * HD, ROWS), FULL),
            pltpu.VMEM((HD, ROWS), FULL),
            pltpu.VMEM((2, 8, ROWS), FULL),
            pltpu.VMEM((2, 8, ROWS), FULL),
            pltpu.VMEM((2, SIDE - 1, LINE, 2 * HD), HALF),
            pltpu.VMEM((2, LINE, 2 * HD), FULL),
            pltpu.VMEM((2, SIDE - 1, LINE, 2 * HD), HALF),
            pltpu.VMEM((2, LINE, 2 * HD), HALF),
            pltpu.VMEM((2, SIDE - 1, CUT, 2 * HD), HALF),
            dma((11,)),
            dma((5,)), dma((5,)),
            dma((slots,)), dma((slots,)),
            dma((slots,)), dma((slots,)),
            dma((slots,)), dma((slots,)),
            dma((slots,)), dma((slots,)),
            dma((slots,)), dma((slots,)),
            dma((2, SIDE - 1)), dma((2, SIDE - 1)),
            dma((2, SIDE - 1)), dma((2, SIDE - 1)),
        ],
        compiler_params=pltpu.CompilerParams(
            collective_id=0, has_side_effects=True, vmem_limit_bytes=60 * 2**20
        ),
    )(timestep, query_in, key_in, value_in, clean_keys, clean_values, mod_table, out_grad)


def solution(mesh):
    assert mesh.shape["tm"] == PLANES and mesh.shape["seq"] == 2 * SIDE * SIDE
    split = P(("tm", "seq"), None)
    return jax.shard_map(
        body,
        mesh=mesh,
        in_specs=(split, split, split, split, split, P("tm"), P(), split),
        out_specs=(split, split, split, split),
        check_vma=False,
    )
```

```python
import math

import jax
import jax.numpy as jnp
from jax import lax
from jax.experimental import pallas as pl
from jax.experimental.pallas import tpu as pltpu
from jax.sharding import PartitionSpec as P

MESH = pl.DeviceIdType.MESH
HALF = jnp.bfloat16
FULL = jnp.float32
SIDE = 4
PLANES = 8
TOK = 128
HD = 128
HEADS = 4
ROWS = HEADS * TOK
BOTH = 2 * ROWS
CUT = TOK // 2
REGION = SIDE * SIDE * CUT
LINE = SIDE * CUT
BK = REGION // 2
MOVED = 3


def dot(a, b):
    return lax.dot_general(a, b, (((1,), (0,)), ((), ())), preferred_element_type=FULL)


def dot_tn(a, b):
    return lax.dot_general(a, b, (((0,), (0,)), ((), ())), preferred_element_type=FULL)


def fold(a, op):
    return op(a.reshape(a.shape[0] // 8, 8, a.shape[1]), axis=0)


def kernel(
    timestep, query, key_in, value_in, clean_keys, clean_values, mod_table, out_grad,
    gated, query_grad, key_grad, value_grad,
    kv, clean, table, grad_in, qg, qg_sib, qg_far, qg_far_sib, qt, gt, q_rows, g_rows,
    s_buf, e_buf, x_buf, m_buf, al_buf, l_buf, m_own, o1, o2,
    ml, ml_sib, o1_sib, o2_sib, far, far_lse, far_out, far_lse_out, stats, stats_sib,
    part, own_part, rs1, rs2_out, rs2,
    in_sem, core_send, core_recv, far_send, far_recv, z_send, z_recv,
    s1_send, s1_recv, up_send, up_recv, down_send, down_recv, s3_send, s3_recv,
    rs1_send, rs1_recv, rs2_send, rs2_recv,
):
    scale = 1.0 / math.sqrt(HD)
    to_log2 = scale * math.log2(math.e)
    z = lax.axis_index("tm")
    seq = lax.axis_index("seq")
    core = lax.rem(seq, 2)
    y = lax.rem(seq // 2, SIDE)
    x = seq // (2 * SIDE)
    helper, helped = z < MOVED, z > PLANES - 1 - MOVED
    partner = (PLANES - 1 - z, seq)
    own_units = jnp.minimum(z, PLANES - 1 - MOVED) + 1
    helped_units = jnp.maximum(MOVED - z, 0)
    gathered = 2 * (own_units + jnp.maximum(MOVED - 2 * z, 0))
    rising = 1 - jnp.minimum(z // 2, 1)
    first_plane = 1 - jnp.minimum(z, 1)

    def region(order):
        i = order // 2
        falling = jnp.minimum(i, 1) * (z + 1 - i)
        ahead = lax.rem(i + first_plane, gathered // 2)
        return 2 * (rising * ahead + (1 - rising) * falling) + lax.rem(order, 2)


    def chip(dx, dy):
        px = lax.rem(x + dx, SIDE)
        py = lax.rem(y + dy, SIDE)
        return (z, (px * SIDE + py) * 2 + core)

    sibling = (z, (x * SIDE + y) * 2 + 1 - core)

    def plane(pz):
        return (pz, seq)

    def remote(src, dst, send, recv, device):
        return pltpu.make_async_remote_copy(
            src_ref=src, dst_ref=dst, send_sem=send, recv_sem=recv,
            device_id=device, device_id_type=MESH,
        )

    def along_line(p, d):
        return chip((1 - p) * d, p * d)

    def across_lines(p, d):
        return chip(p * d, (1 - p) * d)

    def place(p):
        return p * x + (1 - p) * y, p * y + (1 - p) * x

    loads = [
        pltpu.make_async_copy(query, qg.at[0], in_sem.at[0]),
        pltpu.make_async_copy(out_grad, grad_in, in_sem.at[1]),
        pltpu.make_async_copy(mod_table, table, in_sem.at[2]),
    ]
    shards = []
    for p in range(2):
        u, v = place(p)
        rows = pl.ds(p * CUT, CUT)
        noisy_at = pl.ds(pl.multiple_of(u * LINE + v * CUT, CUT), CUT)
        for at, (noisy_in, clean_in) in enumerate(
            ((value_in, clean_values), (key_in, clean_keys))
        ):
            cols = pl.ds(at * HD, HD)
            sem = 3 + 4 * p + 2 * at
            shards.append(
                pltpu.make_async_copy(
                    noisy_in.at[rows, :], kv.at[p, noisy_at, cols], in_sem.at[sem]
                )
            )
            shards.append(
                pltpu.make_async_copy(
                    clean_in.at[rows, :], clean.at[p, :, cols], in_sem.at[sem + 1]
                )
            )
    for load in shards + loads:
        load.start()

    barrier = pltpu.get_barrier_semaphore()
    for d in range(1, SIDE):
        pl.semaphore_signal(barrier, inc=1, device_id=chip(d, 0), device_id_type=MESH)
        pl.semaphore_signal(barrier, inc=1, device_id=chip(0, d), device_id_type=MESH)
    for d in range(1, PLANES):
        pl.semaphore_signal(
            barrier, inc=1, device_id=plane(lax.rem(z + d, PLANES)), device_id_type=MESH
        )
    pl.semaphore_signal(barrier, inc=1, device_id=sibling, device_id_type=MESH)
    for load in shards:
        load.wait()
    pl.semaphore_wait(barrier, 2 * (SIDE - 1) + PLANES)

    def arrived(block, sem):
        pltpu.make_async_copy(block, block, sem).wait()

    def piece_at(r):
        u, v = place(lax.rem(r, 2))
        return kv.at[r, pl.ds(pl.multiple_of(u * LINE + v * CUT, CUT), CUT)]

    def gather_line(r):
        piece = piece_at(r)
        for d in range(1, SIDE):
            remote(
                piece, piece, s1_send.at[r], s1_recv.at[r], along_line(lax.rem(r, 2), d)
            ).start()

    @pl.when(2 * z < MOVED)
    def _():
        for p in range(2):
            r = 2 * jnp.minimum(z + 1, MOVED) + p
            u, v = place(p)
            at = pl.ds(pl.multiple_of(u * LINE + v * CUT, CUT), CUT)
            kv[r, at, :] = clean[p]

    for p in range(2):
        gather_line(region(p))

    def line_at(r, shift):
        u, _ = place(lax.rem(r, 2))
        line = lax.rem(u + shift, SIDE)
        return kv.at[r, pl.ds(pl.multiple_of(line * LINE, LINE), LINE)]

    def half_line_at(r, shift, second):
        u, _ = place(lax.rem(r, 2))
        line = lax.rem(u + shift, SIDE)
        return kv.at[r, pl.ds(pl.multiple_of(line * LINE + second * (LINE // 2), LINE // 2), LINE // 2)]

    def spread(r):
        p = lax.rem(r, 2)
        line = line_at(r, 0)
        remote(line, line, up_send.at[r], up_recv.at[r], across_lines(p, 1)).start()
        remote(line, line, down_send.at[r], down_recv.at[r], across_lines(p, SIDE - 1)).start()

    def pass_on(r):
        p = lax.rem(r, 2)
        arrived(line_at(r, SIDE - 1), up_recv.at[r])
        first = half_line_at(r, SIDE - 1, 0)
        remote(first, first, s3_send.at[r], s3_recv.at[r], across_lines(p, 1)).start()
        arrived(line_at(r, 1), down_recv.at[r])
        second = half_line_at(r, 1, 1)
        remote(second, second, s3_send.at[r], s3_recv.at[r], across_lines(p, SIDE - 1)).start()

    def complete(r):
        arrived(line_at(r, 2), s3_recv.at[r])

    def shard_copy(p, d, pz):
        return remote(
            clean.at[p], piece_at(2 * jnp.minimum(z + 1, PLANES - 1) + p),
            z_send.at[2 * d + p], z_recv.at[2 * jnp.minimum(z + 1, PLANES - 1) + p], plane(pz),
        )

    def each_shard(low, high, act):
        def one(d, carry):
            @pl.when(z + d < PLANES)
            def _():
                for p in range(2):
                    act(shard_copy(p, d, lax.rem(z + d, PLANES)))
            return carry

        lax.fori_loop(low, high, one, 0)

    def left_shard(act):
        @pl.when((z > 0) & (z < MOVED))
        def _():
            for p in range(2):
                act(shard_copy(p, 0, 0))

    def start(copy):
        copy.start()

    def wait_send(copy):
        copy.wait_send()

    def take_shard(r):
        @pl.when((r > 1) & (r // 2 != z + 1))
        def _():
            arrived(piece_at(r), z_recv.at[r])
        gather_line(r)

    def take_line(r):
        arrived(kv.at[r, pl.ds(0, (SIDE - 1) * CUT)], s1_recv.at[r])
        spread(r)

    each_shard(1, 2, start)
    left_shard(start)

    for load in loads:
        load.wait()
    gain = table[pl.ds(timestep[0], 1), :]
    qg[1] = (gain * grad_in[...].astype(FULL)).astype(HALF)
    share_rows = remote(qg, qg_sib, core_send.at[0], core_recv.at[0], sibling)
    share_rows.start()
    far_rows = remote(qg, qg_far, far_send.at[0], far_recv.at[0], partner)
    pass_rows = remote(qg_far, qg_far_sib, core_send.at[2], core_recv.at[2], sibling)

    @pl.when(z == PLANES - 1)
    def _():
        far_rows.start()

    def pass_far_rows():
        far_rows.wait_recv()
        pass_rows.start()


    def lay_rows(source, task, at):
        for h in range(HEADS):
            cols = pl.ds(h * HD, HD)
            rows = pl.ds(at + h * TOK, TOK)
            q_head = source[0, :, cols]
            g_head = source[1, :, cols]
            if task == 0:
                q_rows[rows, :] = q_head
                g_rows[rows, :] = g_head
            qt[task, :, rows] = q_head.T
            gt[task, :, rows] = g_head.T

    each_shard(2, 3, start)
    lay_rows(qg, 0, 0)
    for p in range(2):
        take_line(region(p))
    each_shard(3, 4, start)
    share_rows.wait_recv()
    lay_rows(qg_sib, 0, ROWS)

    def lead(low, high, work):
        def one(order, carry):
            @pl.when(order < gathered)
            def _():
                work(region(order))
            return carry

        lax.fori_loop(low, high, one, 0)

    def first_block(t):
        r, h = region(t - lax.rem(t, 2)), lax.rem(t, 2)
        return (r + h, h), (r + 1, 3 * h)

    def second_block(t):
        r, h = region(t - lax.rem(t, 2)), lax.rem(t, 2)
        return (r, 1 + h), (r + h, 3 - h)

    def rows_of(block, cols):
        return jnp.concatenate([line_at(r, shift)[:, cols] for r, shift in block], axis=0)

    values, keys, all_cols = slice(0, HD), slice(HD, 2 * HD), slice(0, 2 * HD)

    def scores(task, block, parity, j):
        cols = pl.ds(j * ROWS, ROWS)
        s = dot(rows_of(block, keys), qt[task, :, cols])
        s_buf[1 - parity, :, cols] = s
        before = m_buf[parity, :, cols]
        top = jnp.max(fold(s, jnp.max), axis=0, keepdims=True) * to_log2
        after = jnp.maximum(before, top)
        m_buf[1 - parity, :, cols] = after
        al_buf[1 - parity, :, cols] = jnp.exp2(before - after)

    def weigh(task, block, parity, j):
        cols = pl.ds(j * ROWS, ROWS)
        e = jnp.exp2(s_buf[parity, :, cols] * to_log2 - m_buf[parity, :1, cols])
        dprob = dot(rows_of(block, values), gt[task, :, cols])
        e_buf[parity, :, cols] = e.astype(HALF)
        x_buf[parity, :, cols] = (e * dprob).astype(HALF)
        l_buf[task, :, cols] = l_buf[task, :, cols] * al_buf[parity, :, cols] + fold(e, jnp.sum)

    def gather_sums(task, block, parity, j):
        cols = pl.ds(j * ROWS, ROWS)
        al = al_buf[parity, :1, cols]
        o1[task, j] = o1[task, j] * al + dot_tn(rows_of(block, all_cols), e_buf[parity, :, cols])
        o2[task, j] = o2[task, j] * al + dot_tn(rows_of(block, keys), x_buf[parity, :, cols])

    def share_sums(task):
        sem = 3 + 4 * task
        pairs = (
            (ml.at[task], ml_sib.at[task]),
            (o1.at[task, 1, pl.ds(0, HD)], o1_sib.at[task, pl.ds(0, HD)]),
            (o1.at[task, 1, pl.ds(HD, HD)], o1_sib.at[task, pl.ds(HD, HD)]),
            (o2.at[task, 1], o2_sib.at[task]),
        )
        return [
            remote(src, dst, core_send.at[sem + n], core_recv.at[sem + n], sibling)
            for n, (src, dst) in enumerate(pairs)
        ]

    def both_cores(task):
        for share in share_sums(task)[:2]:
            share.wait_recv()
        peak_a = m_own[task, :1, :]
        peak_b = ml_sib[task, 0, :1, :]
        peak = jnp.maximum(peak_a, peak_b)
        part_a = jnp.exp2(peak_a - peak)
        part_b = jnp.exp2(peak_b - peak)
        total = part_a * jnp.sum(l_buf[task, :, :ROWS], axis=0, keepdims=True) + part_b * jnp.sum(
            ml_sib[task, 1], axis=0, keepdims=True
        )
        return peak, total, part_a / total, part_b / total

    far_sums = [
        remote(far_lse_out, far_lse, far_send.at[1], far_recv.at[1], partner),
        remote(
            far_out.at[pl.ds(0, HD)], far.at[pl.ds(0, HD)], far_send.at[2], far_recv.at[2], partner
        ),
        remote(
            far_out.at[pl.ds(HD, 2 * HD)], far.at[pl.ds(HD, 2 * HD)],
            far_send.at[3], far_recv.at[3], partner,
        ),
    ]

    def run(turn, carry):
        task = first_plane * (1 - turn) + (1 - first_plane) * turn
        begin = turn * 2 * (first_plane * MOVED + (1 - first_plane) * own_units)
        first = 2 * (first_plane * (1 - task) * MOVED + (1 - first_plane) * task * jnp.maximum(z, 1))
        end = first + (1 - task) * 2 * own_units + task * 2 * helped_units

        l_buf[task] = jnp.zeros_like(l_buf[task])
        o1[task] = jnp.zeros_like(o1[task])
        o2[task] = jnp.zeros_like(o2[task])
        e_buf[1] = jnp.zeros_like(e_buf[1])
        x_buf[1] = jnp.zeros_like(x_buf[1])
        al_buf[...] = jnp.ones_like(al_buf)
        m_buf[...] = jnp.full_like(m_buf, -1e30)

        def start_gathers():
            for p in range(2):
                pass_on(region(p))
            each_shard(4, PLANES - MOVED, start)

            @pl.when(helped & (z < PLANES - 1))
            def _():
                far_rows.start()

            lead(2, 4, take_line)

        @pl.when(turn == 0)
        def _():
            lead(2, 6, take_shard)

            @pl.when(z == 0)
            def _():
                start_gathers()
                pass_far_rows()

        @pl.when(task == 1)
        def _():
            lay_rows(qg_far, 1, 0)
            pass_rows.wait_recv()
            lay_rows(qg_far_sib, 1, ROWS)

        for j in range(2):
            scores(task, first_block(first), 1, j)

        @pl.when((turn == 0) & (z > 0))
        def _():
            start_gathers()

        def half_step(t, h, j):
            if h == 0:
                weigh(task, first_block(t), 0, j)
                gather_sums(task, second_block(jnp.maximum(t - 1, first)), 1, j)
                scores(task, second_block(t), 0, j)
            else:
                weigh(task, second_block(t), 1, j)
                gather_sums(task, first_block(t), 0, j)
                scores(task, first_block(jnp.minimum(t + 1, end - 1)), 1, j)

        def finish_unit(t):
            done = t - first + begin

            @pl.when((lax.rem(done, 2) == 1) & (done < gathered))
            def _():
                complete(region(done - 1))
                complete(region(done))

        def run_ahead(t):
            n = t - first + begin
            lead(n + 8 - 2 * jnp.maximum(1 - n, 0), n + 9, take_shard)
            lead(jnp.minimum(2 * n + 4, n + 6), jnp.minimum(2 * n + 6, n + 7), take_line)
            lead(
                jnp.maximum(jnp.minimum(2 * n, n + 3), 2), jnp.minimum(2 * n + 2, n + 4), pass_on
            )

        def step(t, inner):
            finish_unit(t)
            for j in range(2):
                half_step(t, 0, j)
            run_ahead(t)
            for j in range(2):
                half_step(t, 1, j)
            return inner

        lax.fori_loop(first, end - 2, step, 0)

        for j in (1, 0):

            def last_step(t, inner):
                if j == 1:
                    finish_unit(t)
                half_step(t, 0, j)
                if j == 1:
                    run_ahead(t)
                half_step(t, 1, j)
                return inner

            lax.fori_loop(end - 2, end, last_step, 0)
            gather_sums(task, second_block(end - 1), 1, j)
            if j == 1:
                ml[task, 0] = m_buf[1, :, ROWS:]
                ml[task, 1] = l_buf[task, :, ROWS:]
                for share in share_sums(task):
                    share.start()

                @pl.when((task == 0) & helper & (z > 0))
                def _():
                    pass_far_rows()
        m_own[task] = m_buf[1, :, :ROWS]

        @pl.when(task == 1)
        def _():
            peak, total, part_a, part_b = both_cores(1)
            far_lse_out[...] = jnp.broadcast_to(peak + jnp.log2(total), (8, ROWS))
            far_out[:HD] = (o1[1, 0, :HD, :] * part_a + o1_sib[1, :HD, :] * part_b).astype(HALF)
            for copy in far_sums[:2]:
                copy.start()
            for share in share_sums(1)[2:]:
                share.wait_recv()
            far_out[HD : 2 * HD] = (o1[1, 0, HD:, :] * part_a + o1_sib[1, HD:, :] * part_b).astype(HALF)
            far_out[2 * HD :] = (o2[1, 0] * part_a + o2_sib[1] * part_b).astype(HALF)
            far_sums[2].start()

        return carry

    lax.fori_loop(0, 2 - jnp.minimum(z // MOVED, 1), run, 0)

    peak, total, part_a, part_b = both_cores(0)
    lse = peak + jnp.log2(total)

    @pl.when(helped)
    def _():
        for copy in far_sums[:2]:
            copy.wait_recv()

    @pl.when(jnp.logical_not(helped))
    def _():
        far[...] = jnp.zeros_like(far)
        far_lse[...] = jnp.full_like(far_lse, -1e30)

    peak = jnp.maximum(lse, far_lse[:1, :])
    part_near = jnp.exp2(lse - peak)
    part_far = jnp.exp2(far_lse[:1, :] - peak)
    total = part_near + part_far
    part_a = part_a * part_near / total
    part_b = part_b * part_near / total
    part_far = part_far / total
    attended = (
        o1[0, 0, :HD, :] * part_a + o1_sib[0, :HD, :] * part_b + far[:HD].astype(FULL) * part_far
    ).astype(HALF)
    delta = jnp.sum(gt[0, :, :ROWS].astype(FULL) * attended.astype(FULL), axis=0, keepdims=True)
    stats[0] = jnp.broadcast_to(peak + jnp.log2(total), (8, ROWS))
    stats[1] = jnp.broadcast_to(delta, (8, ROWS))
    share_stats = remote(stats, stats_sib, core_send.at[1], core_recv.at[1], sibling)
    share_stats.start()

    def backward(p, line, cols, lse, drop):
        block = kv[p, pl.ds(pl.multiple_of(line * LINE, LINE), LINE), :]
        prob = jnp.exp2(dot(block[:, HD:], qt[0, :, cols]) * to_log2 - lse)
        dprob = dot(block[:, :HD], gt[0, :, cols])
        dscore = (prob * (dprob - drop) * scale).astype(HALF)
        vgrad = dot(prob.astype(HALF), g_rows[cols, :])
        kgrad = dot(dscore, q_rows[cols, :])
        return vgrad, kgrad

    def backward_mine(p, line):
        return backward(p, line, pl.ds(0, ROWS), stats[0, :1, :], stats[1, :1, :])

    def backward_theirs(p, line):
        return backward(p, line, pl.ds(ROWS, ROWS), stats_sib[0, :1, :], stats_sib[1, :1, :])

    def backward_all(p, line):
        lse = jnp.concatenate([stats[0, :1, :], stats_sib[0, :1, :]], axis=1)
        drop = jnp.concatenate([stats[1, :1, :], stats_sib[1, :1, :]], axis=1)
        return backward(p, line, pl.ds(0, BOTH), lse, drop)

    def part_copy(p, d):
        return remote(
            part.at[p, d - 1], rs1.at[p, d - 1],
            rs1_send.at[p, d - 1], rs1_recv.at[p, d - 1], across_lines(p, d),
        )

    early = [backward_mine(p, lax.rem(place(p)[0] + 2, SIDE)) for p in range(2)]
    share_stats.wait_recv()
    for d in (2, 1, 3):
        for p in range(2):
            line = lax.rem(place(p)[0] + d, SIDE)
            if d == 2:
                late = backward_theirs(p, line)
                vgrad, kgrad = early[p][0] + late[0], early[p][1] + late[1]
            else:
                vgrad, kgrad = backward_all(p, line)
            part[p, d - 1, :, :HD] = vgrad.astype(HALF)
            part[p, d - 1, :, HD:] = kgrad.astype(HALF)
            part_copy(p, d).start()
    for p in range(2):
        u, _ = place(p)
        vgrad, kgrad = backward_all(p, u)
        own_part[p, :, :HD] = vgrad
        own_part[p, :, HD:] = kgrad

    attended = attended.astype(FULL)
    for h in range(HEADS):
        cols = slice(h * HD, (h + 1) * HD)
        gated[:, cols] = gain[:, cols] * attended[:, h * TOK : (h + 1) * TOK].T

    def piece_copy(p, d):
        _, v = place(p)
        at = pl.multiple_of(lax.rem(v + d, SIDE) * CUT, CUT)
        return remote(
            rs2_out.at[p, pl.ds(at, CUT)], rs2.at[p, d - 1],
            rs2_send.at[p, d - 1], rs2_recv.at[p, d - 1], along_line(p, d),
        )

    for p in range(2):
        for d in range(1, SIDE):
            part_copy(p, d).wait_recv()
        own_part[p] = (
            own_part[p] + rs1[p, 0].astype(FULL) + rs1[p, 1].astype(FULL) + rs1[p, 2].astype(FULL)
        )
        rs2_out[p] = own_part[p].astype(HALF)
        for d in range(1, SIDE):
            piece_copy(p, d).start()

    for share in share_sums(0)[2:]:
        share.wait_recv()

    @pl.when(helped)
    def _():
        far_sums[2].wait_recv()

    mean_key = (
        o1[0, 0, HD:, :] * part_a
        + o1_sib[0, HD:, :] * part_b
        + far[HD : 2 * HD].astype(FULL) * part_far
    )
    qgrad = (
        o2[0, 0] * part_a
        + o2_sib[0] * part_b
        + far[2 * HD :].astype(FULL) * part_far
        - delta * mean_key
    ) * scale
    for h in range(HEADS):
        cols = slice(h * HD, (h + 1) * HD)
        query_grad[:, cols] = qgrad[:, h * TOK : (h + 1) * TOK].T

    for p in range(2):
        _, v = place(p)
        for d in range(1, SIDE):
            piece_copy(p, d).wait_recv()
        mine = own_part[p, pl.ds(pl.multiple_of(v * CUT, CUT), CUT), :]
        mine = mine + rs2[p, 0].astype(FULL) + rs2[p, 1].astype(FULL) + rs2[p, 2].astype(FULL)
        value_grad[pl.ds(p * CUT, CUT), :] = mine[:, :HD]
        key_grad[pl.ds(p * CUT, CUT), :] = mine[:, HD:]

    for copy in [share_rows, share_stats] + share_sums(0):
        copy.wait_send()

    @pl.when(helped)
    def _():
        far_rows.wait_send()

    @pl.when(helper)
    def _():
        for copy in [pass_rows] + share_sums(1) + far_sums:
            copy.wait_send()

    for p in range(2):
        for d in range(1, SIDE):
            part_copy(p, d).wait_send()
            piece_copy(p, d).wait_send()

    def drain(order, carry):
        r = region(order)
        line = line_at(r, 0)
        for sem in (up_send, down_send, s3_send):
            arrived(line, sem.at[r])
        arrived(kv.at[r, pl.ds(0, (SIDE - 1) * CUT)], s1_send.at[r])
        return carry

    lax.fori_loop(0, gathered, drain, 0)
    each_shard(1, PLANES - MOVED, wait_send)
    left_shard(wait_send)


def body(query_in, key_in, value_in, clean_keys, clean_values, timestep, mod_table, out_grad):
    vmem = pl.BlockSpec(memory_space=pltpu.VMEM)
    dma = pltpu.SemaphoreType.DMA
    slots = 2 * PLANES
    return pl.pallas_call(
        kernel,
        name="attend",
        out_shape=[
            jax.ShapeDtypeStruct((TOK, HEADS * HD), FULL),
            jax.ShapeDtypeStruct((TOK, HEADS * HD), FULL),
            jax.ShapeDtypeStruct((TOK, HD), FULL),
            jax.ShapeDtypeStruct((TOK, HD), FULL),
        ],
        in_specs=[pl.BlockSpec(memory_space=pltpu.SMEM)]
        + [pl.BlockSpec(memory_space=pl.ANY)] * 7,
        out_specs=[vmem] * 4,
        scratch_shapes=[
            pltpu.VMEM((slots, REGION, 2 * HD), HALF),
            pltpu.VMEM((2, CUT, 2 * HD), HALF),
            pltpu.VMEM(mod_table.shape, FULL),
            pltpu.VMEM((TOK, HEADS * HD), HALF),
            pltpu.VMEM((2, TOK, HEADS * HD), HALF),
            pltpu.VMEM((2, TOK, HEADS * HD), HALF),
            pltpu.VMEM((2, TOK, HEADS * HD), HALF),
            pltpu.VMEM((2, TOK, HEADS * HD), HALF),
            pltpu.VMEM((2, HD, BOTH), HALF),
            pltpu.VMEM((2, HD, BOTH), HALF),
            pltpu.VMEM((BOTH, HD), HALF),
            pltpu.VMEM((BOTH, HD), HALF),
            pltpu.VMEM((2, BK, BOTH), FULL),
            pltpu.VMEM((2, BK, BOTH), HALF),
            pltpu.VMEM((2, BK, BOTH), HALF),
            pltpu.VMEM((2, 8, BOTH), FULL),
            pltpu.VMEM((2, 8, BOTH), FULL),
            pltpu.VMEM((2, 8, BOTH), FULL),
            pltpu.VMEM((2, 8, ROWS), FULL),
            pltpu.VMEM((2, 2, 2 * HD, ROWS), FULL),
            pltpu.VMEM((2, 2, HD, ROWS), FULL),
            pltpu.VMEM((2, 2, 8, ROWS), FULL),
            pltpu.VMEM((2, 2, 8, ROWS), FULL),
            pltpu.VMEM((2, 2 * HD, ROWS), FULL),
            pltpu.VMEM((2, HD, ROWS), FULL),
            pltpu.VMEM((3 * HD, ROWS), HALF),
            pltpu.VMEM((8, ROWS), FULL),
            pltpu.VMEM((3 * HD, ROWS), HALF),
            pltpu.VMEM((8, ROWS), FULL),
            pltpu.VMEM((2, 8, ROWS), FULL),
            pltpu.VMEM((2, 8, ROWS), FULL),
            pltpu.VMEM((2, SIDE - 1, LINE, 2 * HD), HALF),
            pltpu.VMEM((2, LINE, 2 * HD), FULL),
            pltpu.VMEM((2, SIDE - 1, LINE, 2 * HD), HALF),
            pltpu.VMEM((2, LINE, 2 * HD), HALF),
            pltpu.VMEM((2, SIDE - 1, CUT, 2 * HD), HALF),
            dma((11,)),
            dma((11,)), dma((11,)),
            dma((4,)), dma((4,)),
            dma((2 * (PLANES - MOVED),)), dma((slots,)),
            dma((slots,)), dma((slots,)),
            dma((slots,)), dma((slots,)),
            dma((slots,)), dma((slots,)),
            dma((slots,)), dma((slots,)),
            dma((2, SIDE - 1)), dma((2, SIDE - 1)),
            dma((2, SIDE - 1)), dma((2, SIDE - 1)),
        ],
        compiler_params=pltpu.CompilerParams(
            collective_id=0, has_side_effects=True, vmem_limit_bytes=60 * 2**20
        ),
    )(timestep, query_in, key_in, value_in, clean_keys, clean_values, mod_table, out_grad)


def solution(mesh):
    assert mesh.shape["tm"] == PLANES and mesh.shape["seq"] == 2 * SIDE * SIDE
    split = P(("tm", "seq"), None)
    return jax.shard_map(
        body,
        mesh=mesh,
        in_specs=(split, split, split, split, split, P("tm"), P(), split),
        out_specs=(split, split, split, split),
        check_vma=False,
    )
```

```python
import math

import jax
import jax.numpy as jnp
from jax import lax
from jax.experimental import pallas as pl
from jax.experimental.pallas import tpu as pltpu
from jax.sharding import PartitionSpec as P

MESH = pl.DeviceIdType.MESH
HALF = jnp.bfloat16
FULL = jnp.float32
SIDE = 4
PLANES = 8
TOK = 128
HD = 128
HEADS = 4
ROWS = HEADS * TOK
BOTH = 2 * ROWS
CUT = TOK // 2
REGION = SIDE * SIDE * CUT
LINE = SIDE * CUT
BK = REGION // 2
MOVED = 3


def dot(a, b):
    return lax.dot_general(a, b, (((1,), (0,)), ((), ())), preferred_element_type=FULL)


def dot_tn(a, b):
    return lax.dot_general(a, b, (((0,), (0,)), ((), ())), preferred_element_type=FULL)


def fold(a, op):
    return op(a.reshape(a.shape[0] // 8, 8, a.shape[1]), axis=0)


def kernel(
    timestep, query, key_in, value_in, clean_keys, clean_values, mod_table, out_grad,
    gated, query_grad, key_grad, value_grad,
    kv, clean, table, grad_in, qg, qg_sib, qg_far, qg_far_sib, qt, gt, q_rows, g_rows,
    s_buf, e_buf, x_buf, m_buf, al_buf, l_buf, m_own, o1, o2,
    ml, ml_sib, o1_sib, o2_sib, far, far_lse, far_out, far_lse_out, stats, stats_sib,
    part, own_part, rs1, rs2_out, rs2,
    in_sem, core_send, core_recv, far_send, far_recv, z_send, z_recv,
    s1_send, s1_recv, up_send, up_recv, down_send, down_recv, s3_send, s3_recv,
    rs1_send, rs1_recv, rs2_send, rs2_recv,
):
    scale = 1.0 / math.sqrt(HD)
    to_log2 = scale * math.log2(math.e)
    z = lax.axis_index("tm")
    seq = lax.axis_index("seq")
    core = lax.rem(seq, 2)
    y = lax.rem(seq // 2, SIDE)
    x = seq // (2 * SIDE)
    helper, helped = z < MOVED, z > PLANES - 1 - MOVED
    partner = (PLANES - 1 - z, seq)
    own_units = jnp.minimum(z, PLANES - 1 - MOVED) + 1
    helped_units = jnp.maximum(MOVED - z, 0)
    gathered = 2 * (own_units + jnp.maximum(MOVED - 2 * z, 0))
    rising = 1 - jnp.minimum(z // 2, 1)
    first_plane = 1 - jnp.minimum(z, 1)

    def region(order):
        i = order // 2
        falling = jnp.minimum(i, 1) * (z + 1 - i)
        ahead = lax.rem(i + first_plane, gathered // 2)
        return 2 * (rising * ahead + (1 - rising) * falling) + lax.rem(order, 2)


    def chip(dx, dy):
        px = lax.rem(x + dx, SIDE)
        py = lax.rem(y + dy, SIDE)
        return (z, (px * SIDE + py) * 2 + core)

    sibling = (z, (x * SIDE + y) * 2 + 1 - core)

    def plane(pz):
        return (pz, seq)

    def remote(src, dst, send, recv, device):
        return pltpu.make_async_remote_copy(
            src_ref=src, dst_ref=dst, send_sem=send, recv_sem=recv,
            device_id=device, device_id_type=MESH,
        )

    def along_line(p, d):
        return chip((1 - p) * d, p * d)

    def across_lines(p, d):
        return chip(p * d, (1 - p) * d)

    def place(p):
        return p * x + (1 - p) * y, p * y + (1 - p) * x

    barrier = pltpu.get_barrier_semaphore()
    for d in range(1, SIDE):
        pl.semaphore_signal(barrier, inc=1, device_id=chip(d, 0), device_id_type=MESH)
        pl.semaphore_signal(barrier, inc=1, device_id=chip(0, d), device_id_type=MESH)
    for d in range(1, PLANES):
        pl.semaphore_signal(
            barrier, inc=1, device_id=plane(lax.rem(z + d, PLANES)), device_id_type=MESH
        )
    pl.semaphore_signal(barrier, inc=1, device_id=sibling, device_id_type=MESH)
    loads = [
        pltpu.make_async_copy(query, qg.at[0], in_sem.at[0]),
        pltpu.make_async_copy(out_grad, grad_in, in_sem.at[1]),
        pltpu.make_async_copy(mod_table, table, in_sem.at[2]),
    ]
    shards = []
    for p in range(2):
        u, v = place(p)
        rows = pl.ds(p * CUT, CUT)
        noisy_at = pl.ds(pl.multiple_of(u * LINE + v * CUT, CUT), CUT)
        for at, (noisy_in, clean_in) in enumerate(
            ((value_in, clean_values), (key_in, clean_keys))
        ):
            cols = pl.ds(at * HD, HD)
            sem = 3 + 4 * p + 2 * at
            shards.append(
                pltpu.make_async_copy(
                    noisy_in.at[rows, :], kv.at[p, noisy_at, cols], in_sem.at[sem]
                )
            )
            shards.append(
                pltpu.make_async_copy(
                    clean_in.at[rows, :], clean.at[p, :, cols], in_sem.at[sem + 1]
                )
            )
    for load in shards + loads:
        load.start()

    for load in shards:
        load.wait()
    pl.semaphore_wait(barrier, 2 * (SIDE - 1) + PLANES)

    def arrived(block, sem):
        pltpu.make_async_copy(block, block, sem).wait()

    def piece_at(r):
        u, v = place(lax.rem(r, 2))
        return kv.at[r, pl.ds(pl.multiple_of(u * LINE + v * CUT, CUT), CUT)]

    def gather_line(r):
        piece = piece_at(r)
        for d in range(1, SIDE):
            remote(
                piece, piece, s1_send.at[r], s1_recv.at[r], along_line(lax.rem(r, 2), d)
            ).start()

    @pl.when(2 * z < MOVED)
    def _():
        for p in range(2):
            r = 2 * jnp.minimum(z + 1, MOVED) + p
            u, v = place(p)
            at = pl.ds(pl.multiple_of(u * LINE + v * CUT, CUT), CUT)
            kv[r, at, :] = clean[p]

    for p in range(2):
        gather_line(region(p))

    def line_at(r, shift):
        u, _ = place(lax.rem(r, 2))
        line = lax.rem(u + shift, SIDE)
        return kv.at[r, pl.ds(pl.multiple_of(line * LINE, LINE), LINE)]

    def half_line_at(r, shift, second):
        u, _ = place(lax.rem(r, 2))
        line = lax.rem(u + shift, SIDE)
        return kv.at[r, pl.ds(pl.multiple_of(line * LINE + second * (LINE // 2), LINE // 2), LINE // 2)]

    def spread(r):
        p = lax.rem(r, 2)
        line = line_at(r, 0)
        remote(line, line, up_send.at[r], up_recv.at[r], across_lines(p, 1)).start()
        remote(line, line, down_send.at[r], down_recv.at[r], across_lines(p, SIDE - 1)).start()

    def pass_on(r):
        p = lax.rem(r, 2)
        arrived(line_at(r, SIDE - 1), up_recv.at[r])
        first = half_line_at(r, SIDE - 1, 0)
        remote(first, first, s3_send.at[r], s3_recv.at[r], across_lines(p, 1)).start()
        arrived(line_at(r, 1), down_recv.at[r])
        second = half_line_at(r, 1, 1)
        remote(second, second, s3_send.at[r], s3_recv.at[r], across_lines(p, SIDE - 1)).start()

    def complete(r):
        arrived(line_at(r, 2), s3_recv.at[r])

    def shard_copy(p, d, pz):
        return remote(
            clean.at[p], piece_at(2 * jnp.minimum(z + 1, PLANES - 1) + p),
            z_send.at[2 * d + p], z_recv.at[2 * jnp.minimum(z + 1, PLANES - 1) + p], plane(pz),
        )

    def each_shard(low, high, act):
        def one(d, carry):
            @pl.when(z + d < PLANES)
            def _():
                for p in range(2):
                    act(shard_copy(p, d, lax.rem(z + d, PLANES)))
            return carry

        lax.fori_loop(low, high, one, 0)

    def left_shard(act):
        @pl.when((z > 0) & (z < MOVED))
        def _():
            for p in range(2):
                act(shard_copy(p, 0, 0))

    def start(copy):
        copy.start()

    def wait_send(copy):
        copy.wait_send()

    def take_shard(r):
        @pl.when((r > 1) & (r // 2 != z + 1))
        def _():
            arrived(piece_at(r), z_recv.at[r])
        gather_line(r)

    def take_line(r):
        arrived(kv.at[r, pl.ds(0, (SIDE - 1) * CUT)], s1_recv.at[r])
        spread(r)

    each_shard(1, 2, start)
    left_shard(start)

    for load in loads:
        load.wait()
    gain = table[pl.ds(timestep[0], 1), :]
    qg[1] = (gain * grad_in[...].astype(FULL)).astype(HALF)
    share_rows = remote(qg, qg_sib, core_send.at[0], core_recv.at[0], sibling)
    share_rows.start()
    far_rows = remote(qg, qg_far, far_send.at[0], far_recv.at[0], partner)
    pass_rows = remote(qg_far, qg_far_sib, core_send.at[2], core_recv.at[2], sibling)

    @pl.when(z == PLANES - 1)
    def _():
        far_rows.start()

    def pass_far_rows():
        far_rows.wait_recv()
        pass_rows.start()


    def lay_rows(source, task, at):
        for h in range(HEADS):
            cols = pl.ds(h * HD, HD)
            rows = pl.ds(at + h * TOK, TOK)
            q_head = source[0, :, cols]
            g_head = source[1, :, cols]
            if task == 0:
                q_rows[rows, :] = q_head
                g_rows[rows, :] = g_head
            qt[task, :, rows] = q_head.T
            gt[task, :, rows] = g_head.T

    each_shard(2, 3, start)
    lay_rows(qg, 0, 0)
    each_shard(3, 4, start)
    for p in range(2):
        take_line(region(p))
    each_shard(4, PLANES - MOVED, start)
    share_rows.wait_recv()
    lay_rows(qg_sib, 0, ROWS)

    def lead(low, high, work):
        def one(order, carry):
            @pl.when(order < gathered)
            def _():
                work(region(order))
            return carry

        lax.fori_loop(low, high, one, 0)

    def first_block(t):
        r, h = region(t - lax.rem(t, 2)), lax.rem(t, 2)
        return (r + h, h), (r + 1, 3 * h)

    def second_block(t):
        r, h = region(t - lax.rem(t, 2)), lax.rem(t, 2)
        return (r, 1 + h), (r + h, 3 - h)

    def rows_of(block, cols):
        return jnp.concatenate([line_at(r, shift)[:, cols] for r, shift in block], axis=0)

    values, keys, all_cols = slice(0, HD), slice(HD, 2 * HD), slice(0, 2 * HD)

    def scores(task, block, parity, j):
        cols = pl.ds(j * ROWS, ROWS)
        s = dot(rows_of(block, keys), qt[task, :, cols])
        s_buf[1 - parity, :, cols] = s
        before = m_buf[parity, :, cols]
        top = jnp.max(fold(s, jnp.max), axis=0, keepdims=True) * to_log2
        after = jnp.maximum(before, top)
        m_buf[1 - parity, :, cols] = after
        al_buf[1 - parity, :, cols] = jnp.exp2(before - after)

    def weigh(task, block, parity, j):
        cols = pl.ds(j * ROWS, ROWS)
        e = jnp.exp2(s_buf[parity, :, cols] * to_log2 - m_buf[parity, :1, cols])
        dprob = dot(rows_of(block, values), gt[task, :, cols])
        e_buf[parity, :, cols] = e.astype(HALF)
        x_buf[parity, :, cols] = (e * dprob).astype(HALF)
        l_buf[task, :, cols] = l_buf[task, :, cols] * al_buf[parity, :, cols] + fold(e, jnp.sum)

    def gather_sums(task, block, parity, j):
        cols = pl.ds(j * ROWS, ROWS)
        al = al_buf[parity, :1, cols]
        o1[task, j] = o1[task, j] * al + dot_tn(rows_of(block, all_cols), e_buf[parity, :, cols])
        o2[task, j] = o2[task, j] * al + dot_tn(rows_of(block, keys), x_buf[parity, :, cols])

    def share_sums(task):
        sem = 3 + 4 * task
        pairs = (
            (ml.at[task], ml_sib.at[task]),
            (o1.at[task, 1, pl.ds(0, HD)], o1_sib.at[task, pl.ds(0, HD)]),
            (o1.at[task, 1, pl.ds(HD, HD)], o1_sib.at[task, pl.ds(HD, HD)]),
            (o2.at[task, 1], o2_sib.at[task]),
        )
        return [
            remote(src, dst, core_send.at[sem + n], core_recv.at[sem + n], sibling)
            for n, (src, dst) in enumerate(pairs)
        ]

    def both_cores(task):
        for share in share_sums(task)[:2]:
            share.wait_recv()
        peak_a = m_own[task, :1, :]
        peak_b = ml_sib[task, 0, :1, :]
        peak = jnp.maximum(peak_a, peak_b)
        part_a = jnp.exp2(peak_a - peak)
        part_b = jnp.exp2(peak_b - peak)
        total = part_a * jnp.sum(l_buf[task, :, :ROWS], axis=0, keepdims=True) + part_b * jnp.sum(
            ml_sib[task, 1], axis=0, keepdims=True
        )
        return peak, total, part_a / total, part_b / total

    far_sums = [
        remote(far_lse_out, far_lse, far_send.at[1], far_recv.at[1], partner),
        remote(
            far_out.at[pl.ds(0, HD)], far.at[pl.ds(0, HD)], far_send.at[2], far_recv.at[2], partner
        ),
        remote(
            far_out.at[pl.ds(HD, 2 * HD)], far.at[pl.ds(HD, 2 * HD)],
            far_send.at[3], far_recv.at[3], partner,
        ),
    ]

    def run(turn, carry):
        task = first_plane * (1 - turn) + (1 - first_plane) * turn
        begin = turn * 2 * (first_plane * MOVED + (1 - first_plane) * own_units)
        first = 2 * (first_plane * (1 - task) * MOVED + (1 - first_plane) * task * jnp.maximum(z, 1))
        end = first + (1 - task) * 2 * own_units + task * 2 * helped_units

        l_buf[task] = jnp.zeros_like(l_buf[task])
        o1[task] = jnp.zeros_like(o1[task])
        o2[task] = jnp.zeros_like(o2[task])
        e_buf[1] = jnp.zeros_like(e_buf[1])
        x_buf[1] = jnp.zeros_like(x_buf[1])
        al_buf[...] = jnp.ones_like(al_buf)
        m_buf[...] = jnp.full_like(m_buf, -1e30)

        def start_gathers():
            for p in range(2):
                pass_on(region(p))

            @pl.when(helped & (z < PLANES - 1))
            def _():
                far_rows.start()

            lead(2, 4, take_line)

        @pl.when(turn == 0)
        def _():
            lead(2, 6, take_shard)

            @pl.when(z == 0)
            def _():
                start_gathers()
                pass_far_rows()

        @pl.when(task == 1)
        def _():
            lay_rows(qg_far, 1, 0)
            pass_rows.wait_recv()
            lay_rows(qg_far_sib, 1, ROWS)

        for j in range(2):
            scores(task, first_block(first), 1, j)

        @pl.when((turn == 0) & (z > 0))
        def _():
            start_gathers()

        def half_step(t, h, j):
            if h == 0:
                weigh(task, first_block(t), 0, j)
                gather_sums(task, second_block(jnp.maximum(t - 1, first)), 1, j)
                scores(task, second_block(t), 0, j)
            else:
                weigh(task, second_block(t), 1, j)
                gather_sums(task, first_block(t), 0, j)
                scores(task, first_block(jnp.minimum(t + 1, end - 1)), 1, j)

        def finish_unit(t):
            done = t - first + begin

            @pl.when((lax.rem(done, 2) == 1) & (done < gathered))
            def _():
                complete(region(done - 1))
                complete(region(done))

        def run_ahead(t):
            n = t - first + begin
            lead(6 + 2 * jnp.minimum(n, 1), 8, take_shard)
            lead(
                jnp.maximum(jnp.minimum(2 * n, n + 3), 2), jnp.minimum(2 * n + 2, n + 4), pass_on
            )
            lead(jnp.minimum(2 * n + 4, n + 5), n + 6, take_line)

        def take_next(t):
            n = t - first + begin
            lead(n + 7 + jnp.maximum(1 - n, 0), n + 8, take_shard)

        def step(t, inner):
            take_next(t)
            finish_unit(t)
            for j in range(2):
                half_step(t, 0, j)
            run_ahead(t)
            for j in range(2):
                half_step(t, 1, j)
            return inner

        lax.fori_loop(first, end - 2, step, 0)

        for j in (1, 0):

            def last_step(t, inner):
                if j == 1:
                    take_next(t)
                    finish_unit(t)
                half_step(t, 0, j)
                if j == 1:
                    run_ahead(t)
                half_step(t, 1, j)
                return inner

            lax.fori_loop(end - 2, end, last_step, 0)
            gather_sums(task, second_block(end - 1), 1, j)
            if j == 1:
                ml[task, 0] = m_buf[1, :, ROWS:]
                ml[task, 1] = l_buf[task, :, ROWS:]
                for share in share_sums(task):
                    share.start()

                @pl.when((task == 0) & helper & (z > 0))
                def _():
                    pass_far_rows()
        m_own[task] = m_buf[1, :, :ROWS]

        @pl.when(task == 1)
        def _():
            peak, total, part_a, part_b = both_cores(1)
            far_lse_out[...] = jnp.broadcast_to(peak + jnp.log2(total), (8, ROWS))
            far_out[:HD] = (o1[1, 0, :HD, :] * part_a + o1_sib[1, :HD, :] * part_b).astype(HALF)
            for copy in far_sums[:2]:
                copy.start()
            for share in share_sums(1)[2:]:
                share.wait_recv()
            far_out[HD : 2 * HD] = (o1[1, 0, HD:, :] * part_a + o1_sib[1, HD:, :] * part_b).astype(HALF)
            far_out[2 * HD :] = (o2[1, 0] * part_a + o2_sib[1] * part_b).astype(HALF)
            far_sums[2].start()

        return carry

    lax.fori_loop(0, 2 - jnp.minimum(z // MOVED, 1), run, 0)

    peak, total, part_a, part_b = both_cores(0)
    lse = peak + jnp.log2(total)

    @pl.when(helped)
    def _():
        for copy in far_sums[:2]:
            copy.wait_recv()

    @pl.when(jnp.logical_not(helped))
    def _():
        far[...] = jnp.zeros_like(far)
        far_lse[...] = jnp.full_like(far_lse, -1e30)

    peak = jnp.maximum(lse, far_lse[:1, :])
    part_near = jnp.exp2(lse - peak)
    part_far = jnp.exp2(far_lse[:1, :] - peak)
    total = part_near + part_far
    part_a = part_a * part_near / total
    part_b = part_b * part_near / total
    part_far = part_far / total
    attended = (
        o1[0, 0, :HD, :] * part_a + o1_sib[0, :HD, :] * part_b + far[:HD].astype(FULL) * part_far
    ).astype(HALF)
    delta = jnp.sum(gt[0, :, :ROWS].astype(FULL) * attended.astype(FULL), axis=0, keepdims=True)
    stats[0] = jnp.broadcast_to(peak + jnp.log2(total), (8, ROWS))
    stats[1] = jnp.broadcast_to(delta, (8, ROWS))
    share_stats = remote(stats, stats_sib, core_send.at[1], core_recv.at[1], sibling)
    share_stats.start()

    def backward(p, line, cols, lse, drop):
        block = kv[p, pl.ds(pl.multiple_of(line * LINE, LINE), LINE), :]
        prob = jnp.exp2(dot(block[:, HD:], qt[0, :, cols]) * to_log2 - lse)
        dprob = dot(block[:, :HD], gt[0, :, cols])
        dscore = (prob * (dprob - drop) * scale).astype(HALF)
        vgrad = dot(prob.astype(HALF), g_rows[cols, :])
        kgrad = dot(dscore, q_rows[cols, :])
        return vgrad, kgrad

    def backward_mine(p, line):
        return backward(p, line, pl.ds(0, ROWS), stats[0, :1, :], stats[1, :1, :])

    def backward_theirs(p, line):
        return backward(p, line, pl.ds(ROWS, ROWS), stats_sib[0, :1, :], stats_sib[1, :1, :])

    def backward_all(p, line):
        lse = jnp.concatenate([stats[0, :1, :], stats_sib[0, :1, :]], axis=1)
        drop = jnp.concatenate([stats[1, :1, :], stats_sib[1, :1, :]], axis=1)
        return backward(p, line, pl.ds(0, BOTH), lse, drop)

    def part_copy(p, d):
        return remote(
            part.at[p, d - 1], rs1.at[p, d - 1],
            rs1_send.at[p, d - 1], rs1_recv.at[p, d - 1], across_lines(p, d),
        )

    early = [backward_mine(p, lax.rem(place(p)[0] + 2, SIDE)) for p in range(2)]
    share_stats.wait_recv()
    for d in (2, 1, 3):
        for p in range(2):
            line = lax.rem(place(p)[0] + d, SIDE)
            if d == 2:
                late = backward_theirs(p, line)
                vgrad, kgrad = early[p][0] + late[0], early[p][1] + late[1]
            else:
                vgrad, kgrad = backward_all(p, line)
            part[p, d - 1, :, :HD] = vgrad.astype(HALF)
            part[p, d - 1, :, HD:] = kgrad.astype(HALF)
            part_copy(p, d).start()
    for p in range(2):
        u, _ = place(p)
        vgrad, kgrad = backward_all(p, u)
        own_part[p, :, :HD] = vgrad
        own_part[p, :, HD:] = kgrad

    attended = attended.astype(FULL)
    for h in range(HEADS):
        cols = slice(h * HD, (h + 1) * HD)
        gated[:, cols] = gain[:, cols] * attended[:, h * TOK : (h + 1) * TOK].T

    def piece_copy(p, d):
        _, v = place(p)
        at = pl.multiple_of(lax.rem(v + d, SIDE) * CUT, CUT)
        return remote(
            rs2_out.at[p, pl.ds(at, CUT)], rs2.at[p, d - 1],
            rs2_send.at[p, d - 1], rs2_recv.at[p, d - 1], along_line(p, d),
        )

    for p in range(2):
        for d in range(1, SIDE):
            part_copy(p, d).wait_recv()
        own_part[p] = (
            own_part[p] + rs1[p, 0].astype(FULL) + rs1[p, 1].astype(FULL) + rs1[p, 2].astype(FULL)
        )
        rs2_out[p] = own_part[p].astype(HALF)
        for d in range(1, SIDE):
            piece_copy(p, d).start()

    for share in share_sums(0)[2:]:
        share.wait_recv()

    @pl.when(helped)
    def _():
        far_sums[2].wait_recv()

    mean_key = (
        o1[0, 0, HD:, :] * part_a
        + o1_sib[0, HD:, :] * part_b
        + far[HD : 2 * HD].astype(FULL) * part_far
    )
    qgrad = (
        o2[0, 0] * part_a
        + o2_sib[0] * part_b
        + far[2 * HD :].astype(FULL) * part_far
        - delta * mean_key
    ) * scale
    for h in range(HEADS):
        cols = slice(h * HD, (h + 1) * HD)
        query_grad[:, cols] = qgrad[:, h * TOK : (h + 1) * TOK].T

    for p in range(2):
        _, v = place(p)
        for d in range(1, SIDE):
            piece_copy(p, d).wait_recv()
        mine = own_part[p, pl.ds(pl.multiple_of(v * CUT, CUT), CUT), :]
        mine = mine + rs2[p, 0].astype(FULL) + rs2[p, 1].astype(FULL) + rs2[p, 2].astype(FULL)
        value_grad[pl.ds(p * CUT, CUT), :] = mine[:, :HD]
        key_grad[pl.ds(p * CUT, CUT), :] = mine[:, HD:]

    for copy in [share_rows, share_stats] + share_sums(0):
        copy.wait_send()

    @pl.when(helped)
    def _():
        far_rows.wait_send()

    @pl.when(helper)
    def _():
        for copy in [pass_rows] + share_sums(1) + far_sums:
            copy.wait_send()

    for p in range(2):
        for d in range(1, SIDE):
            part_copy(p, d).wait_send()
            piece_copy(p, d).wait_send()

    def drain(order, carry):
        r = region(order)
        line = line_at(r, 0)
        for sem in (up_send, down_send, s3_send):
            arrived(line, sem.at[r])
        arrived(kv.at[r, pl.ds(0, (SIDE - 1) * CUT)], s1_send.at[r])
        return carry

    lax.fori_loop(0, gathered, drain, 0)
    each_shard(1, PLANES - MOVED, wait_send)
    left_shard(wait_send)


def hand_over(*refs):
    count = len(refs) // 2
    for source, target in zip(refs[:count], refs[count:]):
        target[...] = source[...]


def body(query_in, key_in, value_in, clean_keys, clean_values, timestep, mod_table, out_grad):
    vmem = pl.BlockSpec(memory_space=pltpu.VMEM)
    dma = pltpu.SemaphoreType.DMA
    slots = 2 * PLANES
    found = pl.pallas_call(
        kernel,
        name="attend",
        out_shape=[
            jax.ShapeDtypeStruct((TOK, HEADS * HD), FULL),
            jax.ShapeDtypeStruct((TOK, HEADS * HD), FULL),
            jax.ShapeDtypeStruct((TOK, HD), FULL),
            jax.ShapeDtypeStruct((TOK, HD), FULL),
        ],
        in_specs=[pl.BlockSpec(memory_space=pltpu.SMEM)]
        + [pl.BlockSpec(memory_space=pl.ANY)] * 7,
        out_specs=[vmem] * 4,
        scratch_shapes=[
            pltpu.VMEM((slots, REGION, 2 * HD), HALF),
            pltpu.VMEM((2, CUT, 2 * HD), HALF),
            pltpu.VMEM(mod_table.shape, FULL),
            pltpu.VMEM((TOK, HEADS * HD), HALF),
            pltpu.VMEM((2, TOK, HEADS * HD), HALF),
            pltpu.VMEM((2, TOK, HEADS * HD), HALF),
            pltpu.VMEM((2, TOK, HEADS * HD), HALF),
            pltpu.VMEM((2, TOK, HEADS * HD), HALF),
            pltpu.VMEM((2, HD, BOTH), HALF),
            pltpu.VMEM((2, HD, BOTH), HALF),
            pltpu.VMEM((BOTH, HD), HALF),
            pltpu.VMEM((BOTH, HD), HALF),
            pltpu.VMEM((2, BK, BOTH), FULL),
            pltpu.VMEM((2, BK, BOTH), HALF),
            pltpu.VMEM((2, BK, BOTH), HALF),
            pltpu.VMEM((2, 8, BOTH), FULL),
            pltpu.VMEM((2, 8, BOTH), FULL),
            pltpu.VMEM((2, 8, BOTH), FULL),
            pltpu.VMEM((2, 8, ROWS), FULL),
            pltpu.VMEM((2, 2, 2 * HD, ROWS), FULL),
            pltpu.VMEM((2, 2, HD, ROWS), FULL),
            pltpu.VMEM((2, 2, 8, ROWS), FULL),
            pltpu.VMEM((2, 2, 8, ROWS), FULL),
            pltpu.VMEM((2, 2 * HD, ROWS), FULL),
            pltpu.VMEM((2, HD, ROWS), FULL),
            pltpu.VMEM((3 * HD, ROWS), HALF),
            pltpu.VMEM((8, ROWS), FULL),
            pltpu.VMEM((3 * HD, ROWS), HALF),
            pltpu.VMEM((8, ROWS), FULL),
            pltpu.VMEM((2, 8, ROWS), FULL),
            pltpu.VMEM((2, 8, ROWS), FULL),
            pltpu.VMEM((2, SIDE - 1, LINE, 2 * HD), HALF),
            pltpu.VMEM((2, LINE, 2 * HD), FULL),
            pltpu.VMEM((2, SIDE - 1, LINE, 2 * HD), HALF),
            pltpu.VMEM((2, LINE, 2 * HD), HALF),
            pltpu.VMEM((2, SIDE - 1, CUT, 2 * HD), HALF),
            dma((11,)),
            dma((11,)), dma((11,)),
            dma((4,)), dma((4,)),
            dma((2 * (PLANES - MOVED),)), dma((slots,)),
            dma((slots,)), dma((slots,)),
            dma((slots,)), dma((slots,)),
            dma((slots,)), dma((slots,)),
            dma((slots,)), dma((slots,)),
            dma((2, SIDE - 1)), dma((2, SIDE - 1)),
            dma((2, SIDE - 1)), dma((2, SIDE - 1)),
        ],
        compiler_params=pltpu.CompilerParams(
            collective_id=0, has_side_effects=True, vmem_limit_bytes=60 * 2**20
        ),
    )(timestep, query_in, key_in, value_in, clean_keys, clean_values, mod_table, out_grad)
    return pl.pallas_call(
        hand_over,
        name="hand_over",
        out_shape=[jax.ShapeDtypeStruct(one.shape, one.dtype) for one in found],
        in_specs=[vmem] * 4,
        out_specs=[vmem] * 4,
    )(*found)


def solution(mesh):
    assert mesh.shape["tm"] == PLANES and mesh.shape["seq"] == 2 * SIDE * SIDE
    split = P(("tm", "seq"), None)
    return jax.shard_map(
        body,
        mesh=mesh,
        in_specs=(split, split, split, split, split, P("tm"), P(), split),
        out_specs=(split, split, split, split),
        check_vma=False,
    )
```

```python
import math

import jax
import jax.numpy as jnp
from jax import lax
from jax.experimental import pallas as pl
from jax.experimental.pallas import tpu as pltpu
from jax.sharding import PartitionSpec as P

MESH = pl.DeviceIdType.MESH
HALF = jnp.bfloat16
FULL = jnp.float32
SIDE = 4
PLANES = 8
TOK = 128
HD = 128
HEADS = 4
ROWS = HEADS * TOK
BOTH = 2 * ROWS
CUT = TOK // 2
REGION = SIDE * SIDE * CUT
LINE = SIDE * CUT
BK = REGION // 2
MOVED = 3


def dot(a, b):
    return lax.dot_general(a, b, (((1,), (0,)), ((), ())), preferred_element_type=FULL)


def dot_tn(a, b):
    return lax.dot_general(a, b, (((0,), (0,)), ((), ())), preferred_element_type=FULL)


def fold(a, op):
    return op(a.reshape(a.shape[0] // 8, 8, a.shape[1]), axis=0)


def kernel(
    timestep, query, key_in, value_in, clean_keys, clean_values, mod_table, out_grad,
    gated, query_grad, key_grad, value_grad,
    kv, clean, table, grad_in, qg, qg_sib, qg_far, qg_far_sib, qt, gt, q_rows, g_rows,
    s_buf, e_buf, x_buf, m_buf, al_buf, l_buf, m_own, o1, o2,
    ml, ml_sib, o1_sib, o2_sib, far, far_lse, far_out, far_lse_out, stats, stats_sib,
    part, own_part, rs1, rs2_out, rs2,
    in_sem, core_send, core_recv, far_send, far_recv, z_send, z_recv,
    s1_send, s1_recv, up_send, up_recv, down_send, down_recv, s3_send, s3_recv,
    rs1_send, rs1_recv, rs2_send, rs2_recv,
):
    scale = 1.0 / math.sqrt(HD)
    to_log2 = scale * math.log2(math.e)
    z = lax.axis_index("tm")
    seq = lax.axis_index("seq")
    core = lax.rem(seq, 2)
    y = lax.rem(seq // 2, SIDE)
    x = seq // (2 * SIDE)
    helper, helped = z < MOVED, z > PLANES - 1 - MOVED
    partner = (PLANES - 1 - z, seq)
    own_units = jnp.minimum(z, PLANES - 1 - MOVED) + 1
    helped_units = jnp.maximum(MOVED - z, 0)
    gathered = 2 * (own_units + jnp.maximum(MOVED - 2 * z, 0))
    rising = 1 - jnp.minimum(z // 2, 1)
    first_plane = 1 - jnp.minimum(z, 1)

    def region(order):
        i = order // 2
        falling = jnp.minimum(i, 1) * (z + 1 - i)
        ahead = lax.rem(i + first_plane, gathered // 2)
        return 2 * (rising * ahead + (1 - rising) * falling) + lax.rem(order, 2)


    def chip(dx, dy):
        px = lax.rem(x + dx, SIDE)
        py = lax.rem(y + dy, SIDE)
        return (z, (px * SIDE + py) * 2 + core)

    sibling = (z, (x * SIDE + y) * 2 + 1 - core)

    def plane(pz):
        return (pz, seq)

    def remote(src, dst, send, recv, device):
        return pltpu.make_async_remote_copy(
            src_ref=src, dst_ref=dst, send_sem=send, recv_sem=recv,
            device_id=device, device_id_type=MESH,
        )

    def along_line(p, d):
        return chip((1 - p) * d, p * d)

    def across_lines(p, d):
        return chip(p * d, (1 - p) * d)

    def place(p):
        return p * x + (1 - p) * y, p * y + (1 - p) * x

    barrier = pltpu.get_barrier_semaphore()
    for d in range(1, SIDE):
        pl.semaphore_signal(barrier, inc=1, device_id=chip(d, 0), device_id_type=MESH)
        pl.semaphore_signal(barrier, inc=1, device_id=chip(0, d), device_id_type=MESH)
    for d in range(1, PLANES):
        pl.semaphore_signal(
            barrier, inc=1, device_id=plane(lax.rem(z + d, PLANES)), device_id_type=MESH
        )
    pl.semaphore_signal(barrier, inc=1, device_id=sibling, device_id_type=MESH)
    loads = [
        pltpu.make_async_copy(query, qg.at[0], in_sem.at[0]),
        pltpu.make_async_copy(out_grad, grad_in, in_sem.at[1]),
        pltpu.make_async_copy(mod_table, table, in_sem.at[2]),
    ]
    shards = []
    for p in range(2):
        u, v = place(p)
        rows = pl.ds(p * CUT, CUT)
        noisy_at = pl.ds(pl.multiple_of(u * LINE + v * CUT, CUT), CUT)
        for at, (noisy_in, clean_in) in enumerate(
            ((value_in, clean_values), (key_in, clean_keys))
        ):
            cols = pl.ds(at * HD, HD)
            sem = 3 + 4 * p + 2 * at
            shards.append(
                pltpu.make_async_copy(
                    noisy_in.at[rows, :], kv.at[p, noisy_at, cols], in_sem.at[sem]
                )
            )
            shards.append(
                pltpu.make_async_copy(
                    clean_in.at[rows, :], clean.at[p, :, cols], in_sem.at[sem + 1]
                )
            )
    for load in shards + loads:
        load.start()

    for load in shards:
        load.wait()
    pl.semaphore_wait(barrier, 2 * (SIDE - 1) + PLANES)

    def arrived(block, sem):
        pltpu.make_async_copy(block, block, sem).wait()

    def piece_at(r):
        u, v = place(lax.rem(r, 2))
        return kv.at[r, pl.ds(pl.multiple_of(u * LINE + v * CUT, CUT), CUT)]

    def gather_line(r):
        piece = piece_at(r)
        for d in range(1, SIDE):
            remote(
                piece, piece, s1_send.at[r], s1_recv.at[r], along_line(lax.rem(r, 2), d)
            ).start()

    @pl.when(2 * z < MOVED)
    def _():
        for p in range(2):
            r = 2 * jnp.minimum(z + 1, MOVED) + p
            u, v = place(p)
            at = pl.ds(pl.multiple_of(u * LINE + v * CUT, CUT), CUT)
            kv[r, at, :] = clean[p]

    for p in range(2):
        gather_line(region(p))

    def line_at(r, shift):
        u, _ = place(lax.rem(r, 2))
        line = lax.rem(u + shift, SIDE)
        return kv.at[r, pl.ds(pl.multiple_of(line * LINE, LINE), LINE)]

    def half_line_at(r, shift, second):
        u, _ = place(lax.rem(r, 2))
        line = lax.rem(u + shift, SIDE)
        return kv.at[r, pl.ds(pl.multiple_of(line * LINE + second * (LINE // 2), LINE // 2), LINE // 2)]

    def spread(r):
        p = lax.rem(r, 2)
        line = line_at(r, 0)
        remote(line, line, up_send.at[r], up_recv.at[r], across_lines(p, 1)).start()
        remote(line, line, down_send.at[r], down_recv.at[r], across_lines(p, SIDE - 1)).start()

    def pass_on(r):
        p = lax.rem(r, 2)
        arrived(line_at(r, SIDE - 1), up_recv.at[r])
        first = half_line_at(r, SIDE - 1, 0)
        remote(first, first, s3_send.at[r], s3_recv.at[r], across_lines(p, 1)).start()
        arrived(line_at(r, 1), down_recv.at[r])
        second = half_line_at(r, 1, 1)
        remote(second, second, s3_send.at[r], s3_recv.at[r], across_lines(p, SIDE - 1)).start()

    def complete(r):
        arrived(line_at(r, 2), s3_recv.at[r])

    def shard_copy(p, d, pz):
        return remote(
            clean.at[p], piece_at(2 * jnp.minimum(z + 1, PLANES - 1) + p),
            z_send.at[2 * d + p], z_recv.at[2 * jnp.minimum(z + 1, PLANES - 1) + p], plane(pz),
        )

    def each_shard(low, high, act):
        def one(d, carry):
            @pl.when(z + d < PLANES)
            def _():
                for p in range(2):
                    act(shard_copy(p, d, lax.rem(z + d, PLANES)))
            return carry

        lax.fori_loop(low, high, one, 0)

    def left_shard(act):
        @pl.when((z > 0) & (z < MOVED))
        def _():
            for p in range(2):
                act(shard_copy(p, 0, 0))

    def start(copy):
        copy.start()

    def wait_send(copy):
        copy.wait_send()

    def take_shard(r):
        @pl.when((r > 1) & (r // 2 != z + 1))
        def _():
            arrived(piece_at(r), z_recv.at[r])
        gather_line(r)

    def take_line(r):
        arrived(kv.at[r, pl.ds(0, (SIDE - 1) * CUT)], s1_recv.at[r])
        spread(r)

    each_shard(1, 2, start)
    left_shard(start)

    for load in loads:
        load.wait()
    gain = table[pl.ds(timestep[0], 1), :]
    qg[1] = (gain * grad_in[...].astype(FULL)).astype(HALF)
    share_rows = remote(qg, qg_sib, core_send.at[0], core_recv.at[0], sibling)
    share_rows.start()
    far_rows = remote(qg, qg_far, far_send.at[0], far_recv.at[0], partner)
    pass_rows = remote(qg_far, qg_far_sib, core_send.at[2], core_recv.at[2], sibling)

    @pl.when(z == PLANES - 1)
    def _():
        far_rows.start()

    def pass_far_rows():
        far_rows.wait_recv()
        pass_rows.start()


    def lay_rows(source, task, at):
        for h in range(HEADS):
            cols = pl.ds(h * HD, HD)
            rows = pl.ds(at + h * TOK, TOK)
            q_head = source[0, :, cols]
            g_head = source[1, :, cols]
            if task == 0:
                q_rows[rows, :] = q_head
                g_rows[rows, :] = g_head
            qt[task, :, rows] = q_head.T
            gt[task, :, rows] = g_head.T

    each_shard(2, 3, start)
    lay_rows(qg, 0, 0)
    each_shard(3, 4, start)
    for p in range(2):
        take_line(region(p))
    each_shard(4, PLANES - MOVED, start)
    share_rows.wait_recv()
    lay_rows(qg_sib, 0, ROWS)

    def lead(low, high, work):
        def one(order, carry):
            @pl.when(order < gathered)
            def _():
                work(region(order))
            return carry

        lax.fori_loop(low, high, one, 0)

    def first_block(t):
        r, h = region(t - lax.rem(t, 2)), lax.rem(t, 2)
        return (r + h, h), (r + 1, 3 * h)

    def second_block(t):
        r, h = region(t - lax.rem(t, 2)), lax.rem(t, 2)
        return (r, 1 + h), (r + h, 3 - h)

    def rows_of(block, cols):
        return jnp.concatenate([line_at(r, shift)[:, cols] for r, shift in block], axis=0)

    values, keys, all_cols = slice(0, HD), slice(HD, 2 * HD), slice(0, 2 * HD)

    def scores(task, block, parity, j):
        cols = pl.ds(j * ROWS, ROWS)
        s = dot(rows_of(block, keys), qt[task, :, cols])
        s_buf[1 - parity, :, cols] = s
        before = m_buf[parity, :, cols]
        top = jnp.max(fold(s, jnp.max), axis=0, keepdims=True) * to_log2
        after = jnp.maximum(before, top)
        m_buf[1 - parity, :, cols] = after
        al_buf[1 - parity, :, cols] = jnp.exp2(before - after)

    def weigh(task, block, parity, j):
        cols = pl.ds(j * ROWS, ROWS)
        e = jnp.exp2(s_buf[parity, :, cols] * to_log2 - m_buf[parity, :1, cols])
        dprob = dot(rows_of(block, values), gt[task, :, cols])
        e_buf[parity, :, cols] = e.astype(HALF)
        x_buf[parity, :, cols] = (e * dprob).astype(HALF)
        l_buf[task, :, cols] = l_buf[task, :, cols] * al_buf[parity, :, cols] + fold(e, jnp.sum)

    def gather_sums(task, block, parity, j):
        cols = pl.ds(j * ROWS, ROWS)
        al = al_buf[parity, :1, cols]
        o1[task, j] = o1[task, j] * al + dot_tn(rows_of(block, all_cols), e_buf[parity, :, cols])
        o2[task, j] = o2[task, j] * al + dot_tn(rows_of(block, keys), x_buf[parity, :, cols])

    def share_sums(task):
        sem = 3 + 4 * task
        pairs = (
            (ml.at[task], ml_sib.at[task]),
            (o1.at[task, 1, pl.ds(0, HD)], o1_sib.at[task, pl.ds(0, HD)]),
            (o1.at[task, 1, pl.ds(HD, HD)], o1_sib.at[task, pl.ds(HD, HD)]),
            (o2.at[task, 1], o2_sib.at[task]),
        )
        return [
            remote(src, dst, core_send.at[sem + n], core_recv.at[sem + n], sibling)
            for n, (src, dst) in enumerate(pairs)
        ]

    def both_cores(task):
        for share in share_sums(task)[:2]:
            share.wait_recv()
        peak_a = m_own[task, :1, :]
        peak_b = ml_sib[task, 0, :1, :]
        peak = jnp.maximum(peak_a, peak_b)
        part_a = jnp.exp2(peak_a - peak)
        part_b = jnp.exp2(peak_b - peak)
        total = part_a * jnp.sum(l_buf[task, :, :ROWS], axis=0, keepdims=True) + part_b * jnp.sum(
            ml_sib[task, 1], axis=0, keepdims=True
        )
        return peak, total, part_a / total, part_b / total

    far_sums = [
        remote(far_lse_out, far_lse, far_send.at[1], far_recv.at[1], partner),
        remote(
            far_out.at[pl.ds(0, HD)], far.at[pl.ds(0, HD)], far_send.at[2], far_recv.at[2], partner
        ),
        remote(
            far_out.at[pl.ds(HD, 2 * HD)], far.at[pl.ds(HD, 2 * HD)],
            far_send.at[3], far_recv.at[3], partner,
        ),
    ]

    def run(turn, carry):
        task = first_plane * (1 - turn) + (1 - first_plane) * turn
        begin = turn * 2 * (first_plane * MOVED + (1 - first_plane) * own_units)
        first = 2 * (first_plane * (1 - task) * MOVED + (1 - first_plane) * task * jnp.maximum(z, 1))
        end = first + (1 - task) * 2 * own_units + task * 2 * helped_units

        l_buf[task] = jnp.zeros_like(l_buf[task])
        o1[task] = jnp.zeros_like(o1[task])
        o2[task] = jnp.zeros_like(o2[task])
        e_buf[1] = jnp.zeros_like(e_buf[1])
        x_buf[1] = jnp.zeros_like(x_buf[1])
        al_buf[...] = jnp.ones_like(al_buf)
        m_buf[...] = jnp.full_like(m_buf, -1e30)

        def start_gathers():
            for p in range(2):
                pass_on(region(p))

            @pl.when(helped & (z < PLANES - 1))
            def _():
                far_rows.start()

            lead(2, 4, take_line)

        @pl.when(turn == 0)
        def _():
            lead(2, 6, take_shard)

            @pl.when(z == 0)
            def _():
                start_gathers()
                pass_far_rows()

        @pl.when(task == 1)
        def _():
            lay_rows(qg_far, 1, 0)
            pass_rows.wait_recv()
            lay_rows(qg_far_sib, 1, ROWS)

        for j in range(2):
            scores(task, first_block(first), 1, j)

        @pl.when((turn == 0) & (z > 0))
        def _():
            start_gathers()

        def half_step(t, h, j, final=False):
            if h == 0:
                weigh(task, first_block(t), 0, j)
                gather_sums(task, second_block(jnp.maximum(t - 1, first)), 1, j)
                scores(task, second_block(t), 0, j)
            else:
                weigh(task, second_block(t), 1, j)
                gather_sums(task, first_block(t), 0, j)
                if not final:
                    scores(task, first_block(jnp.minimum(t + 1, end - 1)), 1, j)

        def finish_unit(t):
            done = t - first + begin

            @pl.when((lax.rem(done, 2) == 1) & (done < gathered))
            def _():
                complete(region(done - 1))
                complete(region(done))

        def run_ahead(t):
            n = t - first + begin
            lead(6 + 2 * jnp.minimum(n, 1), 8, take_shard)
            lead(
                jnp.maximum(jnp.minimum(2 * n, n + 3), 2), jnp.minimum(2 * n + 2, n + 4), pass_on
            )
            lead(jnp.minimum(2 * n + 4, n + 5), n + 6, take_line)

        def take_next(t):
            n = t - first + begin
            lead(n + 7 + jnp.maximum(1 - n, 0), n + 8, take_shard)

        def step(t, inner):
            take_next(t)
            finish_unit(t)
            for j in range(2):
                half_step(t, 0, j)
            run_ahead(t)
            for j in range(2):
                half_step(t, 1, j)
            return inner

        lax.fori_loop(first, end - 2, step, 0)

        for j in (1, 0):
            for back in (2, 1):
                t = end - back
                if j == 1:
                    take_next(t)
                    finish_unit(t)
                half_step(t, 0, j)
                if j == 1:
                    run_ahead(t)
                half_step(t, 1, j, final=back == 1)
            gather_sums(task, second_block(end - 1), 1, j)
            if j == 1:
                ml[task, 0] = m_buf[1, :, ROWS:]
                ml[task, 1] = l_buf[task, :, ROWS:]
                for share in share_sums(task):
                    share.start()

                @pl.when((task == 0) & helper & (z > 0))
                def _():
                    pass_far_rows()
        m_own[task] = m_buf[1, :, :ROWS]

        @pl.when(task == 1)
        def _():
            peak, total, part_a, part_b = both_cores(1)
            far_lse_out[...] = jnp.broadcast_to(peak + jnp.log2(total), (8, ROWS))
            far_out[:HD] = (o1[1, 0, :HD, :] * part_a + o1_sib[1, :HD, :] * part_b).astype(HALF)
            for copy in far_sums[:2]:
                copy.start()
            for share in share_sums(1)[2:]:
                share.wait_recv()
            far_out[HD : 2 * HD] = (o1[1, 0, HD:, :] * part_a + o1_sib[1, HD:, :] * part_b).astype(HALF)
            far_out[2 * HD :] = (o2[1, 0] * part_a + o2_sib[1] * part_b).astype(HALF)
            far_sums[2].start()

        return carry

    lax.fori_loop(0, 2 - jnp.minimum(z // MOVED, 1), run, 0)

    peak, total, part_a, part_b = both_cores(0)
    lse = peak + jnp.log2(total)

    @pl.when(helped)
    def _():
        for copy in far_sums[:2]:
            copy.wait_recv()

    @pl.when(jnp.logical_not(helped))
    def _():
        far[...] = jnp.zeros_like(far)
        far_lse[...] = jnp.full_like(far_lse, -1e30)

    peak = jnp.maximum(lse, far_lse[:1, :])
    part_near = jnp.exp2(lse - peak)
    part_far = jnp.exp2(far_lse[:1, :] - peak)
    total = part_near + part_far
    part_a = part_a * part_near / total
    part_b = part_b * part_near / total
    part_far = part_far / total
    attended = (
        o1[0, 0, :HD, :] * part_a + o1_sib[0, :HD, :] * part_b + far[:HD].astype(FULL) * part_far
    ).astype(HALF)
    delta = jnp.sum(gt[0, :, :ROWS].astype(FULL) * attended.astype(FULL), axis=0, keepdims=True)
    stats[0] = jnp.broadcast_to(peak + jnp.log2(total), (8, ROWS))
    stats[1] = jnp.broadcast_to(delta, (8, ROWS))
    share_stats = remote(stats, stats_sib, core_send.at[1], core_recv.at[1], sibling)
    share_stats.start()

    def backward(p, line, cols, lse, drop):
        block = kv[p, pl.ds(pl.multiple_of(line * LINE, LINE), LINE), :]
        prob = jnp.exp2(dot(block[:, HD:], qt[0, :, cols]) * to_log2 - lse)
        dprob = dot(block[:, :HD], gt[0, :, cols])
        dscore = (prob * (dprob - drop) * scale).astype(HALF)
        vgrad = dot(prob.astype(HALF), g_rows[cols, :])
        kgrad = dot(dscore, q_rows[cols, :])
        return vgrad, kgrad

    def backward_mine(p, line):
        return backward(p, line, pl.ds(0, ROWS), stats[0, :1, :], stats[1, :1, :])

    def backward_theirs(p, line):
        return backward(p, line, pl.ds(ROWS, ROWS), stats_sib[0, :1, :], stats_sib[1, :1, :])

    def backward_all(p, line):
        lse = jnp.concatenate([stats[0, :1, :], stats_sib[0, :1, :]], axis=1)
        drop = jnp.concatenate([stats[1, :1, :], stats_sib[1, :1, :]], axis=1)
        return backward(p, line, pl.ds(0, BOTH), lse, drop)

    def part_copy(p, d):
        return remote(
            part.at[p, d - 1], rs1.at[p, d - 1],
            rs1_send.at[p, d - 1], rs1_recv.at[p, d - 1], across_lines(p, d),
        )

    early = [backward_mine(p, lax.rem(place(p)[0] + 2, SIDE)) for p in range(2)]
    share_stats.wait_recv()
    for d in (2, 1, 3):
        for p in range(2):
            line = lax.rem(place(p)[0] + d, SIDE)
            if d == 2:
                late = backward_theirs(p, line)
                vgrad, kgrad = early[p][0] + late[0], early[p][1] + late[1]
            else:
                vgrad, kgrad = backward_all(p, line)
            part[p, d - 1, :, :HD] = vgrad.astype(HALF)
            part[p, d - 1, :, HD:] = kgrad.astype(HALF)
            part_copy(p, d).start()
    for p in range(2):
        u, _ = place(p)
        vgrad, kgrad = backward_all(p, u)
        own_part[p, :, :HD] = vgrad
        own_part[p, :, HD:] = kgrad

    attended = attended.astype(FULL)
    for h in range(HEADS):
        cols = slice(h * HD, (h + 1) * HD)
        gated[:, cols] = gain[:, cols] * attended[:, h * TOK : (h + 1) * TOK].T

    def piece_copy(p, d):
        _, v = place(p)
        at = pl.multiple_of(lax.rem(v + d, SIDE) * CUT, CUT)
        return remote(
            rs2_out.at[p, pl.ds(at, CUT)], rs2.at[p, d - 1],
            rs2_send.at[p, d - 1], rs2_recv.at[p, d - 1], along_line(p, d),
        )

    for p in range(2):
        for d in range(1, SIDE):
            part_copy(p, d).wait_recv()
        own_part[p] = (
            own_part[p] + rs1[p, 0].astype(FULL) + rs1[p, 1].astype(FULL) + rs1[p, 2].astype(FULL)
        )
        rs2_out[p] = own_part[p].astype(HALF)
        for d in range(1, SIDE):
            piece_copy(p, d).start()

    for share in share_sums(0)[2:]:
        share.wait_recv()

    @pl.when(helped)
    def _():
        far_sums[2].wait_recv()

    mean_key = (
        o1[0, 0, HD:, :] * part_a
        + o1_sib[0, HD:, :] * part_b
        + far[HD : 2 * HD].astype(FULL) * part_far
    )
    qgrad = (
        o2[0, 0] * part_a
        + o2_sib[0] * part_b
        + far[2 * HD :].astype(FULL) * part_far
        - delta * mean_key
    ) * scale
    for h in range(HEADS):
        cols = slice(h * HD, (h + 1) * HD)
        query_grad[:, cols] = qgrad[:, h * TOK : (h + 1) * TOK].T

    for p in range(2):
        _, v = place(p)
        for d in range(1, SIDE):
            piece_copy(p, d).wait_recv()
        mine = own_part[p, pl.ds(pl.multiple_of(v * CUT, CUT), CUT), :]
        mine = mine + rs2[p, 0].astype(FULL) + rs2[p, 1].astype(FULL) + rs2[p, 2].astype(FULL)
        value_grad[pl.ds(p * CUT, CUT), :] = mine[:, :HD]
        key_grad[pl.ds(p * CUT, CUT), :] = mine[:, HD:]

    for copy in [share_rows, share_stats] + share_sums(0):
        copy.wait_send()

    @pl.when(helped)
    def _():
        far_rows.wait_send()

    @pl.when(helper)
    def _():
        for copy in [pass_rows] + share_sums(1) + far_sums:
            copy.wait_send()

    for p in range(2):
        for d in range(1, SIDE):
            part_copy(p, d).wait_send()
            piece_copy(p, d).wait_send()

    def drain(order, carry):
        r = region(order)
        line = line_at(r, 0)
        for sem in (up_send, down_send, s3_send):
            arrived(line, sem.at[r])
        arrived(kv.at[r, pl.ds(0, (SIDE - 1) * CUT)], s1_send.at[r])
        return carry

    lax.fori_loop(0, gathered, drain, 0)
    each_shard(1, PLANES - MOVED, wait_send)
    left_shard(wait_send)


def hand_over(*refs):
    count = len(refs) // 2
    for source, target in zip(refs[:count], refs[count:]):
        target[...] = source[...]


def body(query_in, key_in, value_in, clean_keys, clean_values, timestep, mod_table, out_grad):
    vmem = pl.BlockSpec(memory_space=pltpu.VMEM)
    dma = pltpu.SemaphoreType.DMA
    slots = 2 * PLANES
    found = pl.pallas_call(
        kernel,
        name="attend",
        out_shape=[
            jax.ShapeDtypeStruct((TOK, HEADS * HD), FULL),
            jax.ShapeDtypeStruct((TOK, HEADS * HD), FULL),
            jax.ShapeDtypeStruct((TOK, HD), FULL),
            jax.ShapeDtypeStruct((TOK, HD), FULL),
        ],
        in_specs=[pl.BlockSpec(memory_space=pltpu.SMEM)]
        + [pl.BlockSpec(memory_space=pl.ANY)] * 7,
        out_specs=[vmem] * 4,
        scratch_shapes=[
            pltpu.VMEM((slots, REGION, 2 * HD), HALF),
            pltpu.VMEM((2, CUT, 2 * HD), HALF),
            pltpu.VMEM(mod_table.shape, FULL),
            pltpu.VMEM((TOK, HEADS * HD), HALF),
            pltpu.VMEM((2, TOK, HEADS * HD), HALF),
            pltpu.VMEM((2, TOK, HEADS * HD), HALF),
            pltpu.VMEM((2, TOK, HEADS * HD), HALF),
            pltpu.VMEM((2, TOK, HEADS * HD), HALF),
            pltpu.VMEM((2, HD, BOTH), HALF),
            pltpu.VMEM((2, HD, BOTH), HALF),
            pltpu.VMEM((BOTH, HD), HALF),
            pltpu.VMEM((BOTH, HD), HALF),
            pltpu.VMEM((2, BK, BOTH), FULL),
            pltpu.VMEM((2, BK, BOTH), HALF),
            pltpu.VMEM((2, BK, BOTH), HALF),
            pltpu.VMEM((2, 8, BOTH), FULL),
            pltpu.VMEM((2, 8, BOTH), FULL),
            pltpu.VMEM((2, 8, BOTH), FULL),
            pltpu.VMEM((2, 8, ROWS), FULL),
            pltpu.VMEM((2, 2, 2 * HD, ROWS), FULL),
            pltpu.VMEM((2, 2, HD, ROWS), FULL),
            pltpu.VMEM((2, 2, 8, ROWS), FULL),
            pltpu.VMEM((2, 2, 8, ROWS), FULL),
            pltpu.VMEM((2, 2 * HD, ROWS), FULL),
            pltpu.VMEM((2, HD, ROWS), FULL),
            pltpu.VMEM((3 * HD, ROWS), HALF),
            pltpu.VMEM((8, ROWS), FULL),
            pltpu.VMEM((3 * HD, ROWS), HALF),
            pltpu.VMEM((8, ROWS), FULL),
            pltpu.VMEM((2, 8, ROWS), FULL),
            pltpu.VMEM((2, 8, ROWS), FULL),
            pltpu.VMEM((2, SIDE - 1, LINE, 2 * HD), HALF),
            pltpu.VMEM((2, LINE, 2 * HD), FULL),
            pltpu.VMEM((2, SIDE - 1, LINE, 2 * HD), HALF),
            pltpu.VMEM((2, LINE, 2 * HD), HALF),
            pltpu.VMEM((2, SIDE - 1, CUT, 2 * HD), HALF),
            dma((11,)),
            dma((11,)), dma((11,)),
            dma((4,)), dma((4,)),
            dma((2 * (PLANES - MOVED),)), dma((slots,)),
            dma((slots,)), dma((slots,)),
            dma((slots,)), dma((slots,)),
            dma((slots,)), dma((slots,)),
            dma((slots,)), dma((slots,)),
            dma((2, SIDE - 1)), dma((2, SIDE - 1)),
            dma((2, SIDE - 1)), dma((2, SIDE - 1)),
        ],
        compiler_params=pltpu.CompilerParams(
            collective_id=0, has_side_effects=True, vmem_limit_bytes=60 * 2**20
        ),
    )(timestep, query_in, key_in, value_in, clean_keys, clean_values, mod_table, out_grad)
    return pl.pallas_call(
        hand_over,
        name="hand_over",
        out_shape=[jax.ShapeDtypeStruct(one.shape, one.dtype) for one in found],
        in_specs=[vmem] * 4,
        out_specs=[vmem] * 4,
    )(*found)


def solution(mesh):
    assert mesh.shape["tm"] == PLANES and mesh.shape["seq"] == 2 * SIDE * SIDE
    split = P(("tm", "seq"), None)
    return jax.shard_map(
        body,
        mesh=mesh,
        in_specs=(split, split, split, split, split, P("tm"), P(), split),
        out_specs=(split, split, split, split),
        check_vma=False,
    )
```
